256 devices in a mesh: dp: 16 (over y, z_lo, core), seq: 16 (over x, z_hi).
Axes of the slice: x: 4, y: 4, z: 8 (z_hi: 4, z_lo: 2; z = z_hi * 2 + z_lo), core: 2. Of those that a mesh axis runs over, the one named last changes fastest.
Arguments:
- x1_pixels: bfloat16 [16, 16, 256, 1152], P('dp', None, 'seq'), may hold values from -400 to 400, as said below
- dout_frames: bfloat16 [16, 16, 256, 1152], P('dp', 'seq'), may hold values from -6 to 6
- w_qkv: bfloat16 [1152, 3456], replicated, may hold values from -0.1875 to 0.1875
- w_out: bfloat16 [1152, 1152], replicated, may hold values from -0.1875 to 0.1875
Outputs:
- d_x1: bfloat16 [16, 16, 256, 1152], P('dp', 'seq')
- g_qkv: float32 [1152, 3456], P('dp', 'seq')
- g_out: float32 [1152, 1152], P('dp', 'seq')
The draws below stay inside these ranges and needn't reach their ends.
Inputs may be any that keep to these rules, and one draw needn't show every extreme that they name: `x1_pixels`: features of a token have unlike scales.
All inputs are finite; a program needn't handle non-finite values.
Results may differ from the reference program's by a relative error of at most 0.0072.
The reference program's roundings to bfloat16 on the way count: a program that leaves them out, or rounds other values in their place, can miss the bound.
Values may be sent and summed in bfloat16 or wider, within the bound.
A program may use at most 192 MiB of HBM per device.

```python
import math
import jax
import jax.numpy as jnp
from jax import lax

D = 1152
HEADS = 16
F = 16
S = 256
CLIPS = 16


def draw_x1_pixels(key, part):
    key = jax.random.fold_in(key, 11)
    key_base, key_row, key_col = jax.random.split(key, 3)
    shape = (CLIPS, F, S, D)
    row_scale = jnp.exp(jax.random.uniform(key_row, (CLIPS, F, S, 1), jnp.float32, 0.0, math.log(10.0)))
    base = jnp.clip(jax.random.normal(key_base, shape, jnp.float32), -4.0, 4.0)
    col_scale = jnp.exp(jax.random.uniform(key_col, (D,), jnp.float32, 0.0, math.log(10.0)))
    return jnp.clip(base * row_scale * col_scale, -400.0, 400.0).astype(jnp.bfloat16)


def with_spikes(entries, rng, source, target, blocks, factor):
    def block_of(axis_at):
        return (jnp.arange(entries.shape[axis_at]) // (entries.shape[axis_at] // blocks)).reshape((-1,) + (1,) * (entries.ndim - 1 - axis_at))

    first = jax.random.permutation(rng, blocks)[block_of(target)]
    second = (block_of(target) + blocks // 2) % blocks
    return jnp.where((block_of(source) == first) | (block_of(source) == second), factor * entries, entries)


def levels(key, dims, cuts, least, largest):
    gain, own = 1.0, jax.random.fold_in(key, 6)
    for axis_at, shards_of in cuts:
        draws = jnp.exp(jax.random.uniform(jax.random.fold_in(own, axis_at), (shards_of,), jnp.float32, least / len(cuts), largest / len(cuts)))
        gain = gain * jnp.repeat(draws, dims[axis_at] // shards_of).reshape([-1 if axis == axis_at else 1 for axis in range(len(dims))])
    return gain


def scatter_about(stream_key, extent, scale, reach, shards=(), dtype=jnp.bfloat16):
    result = scale * jax.random.normal(stream_key, extent, jnp.float32)
    if shards:
        result = result * levels(stream_key, extent, shards, -0.22, 0.18)
    return jnp.clip(result, -reach, reach).astype(dtype)


def gaussian_with(stream_key, extent, spread, reach, cuts, heavy, dtype=jnp.bfloat16):
    entries = spread * jax.random.normal(stream_key, extent, jnp.float32)
    if cuts:
        entries = entries * levels(stream_key, extent, cuts, -0.22, 0.18)
    return jnp.clip(with_spikes(entries, jax.random.fold_in(stream_key, 3), *heavy), -reach, reach).astype(dtype)


def setup_inputs(seed: int = 0) -> dict:
    arg_keys = jax.random.split(jax.random.key(seed), 5)
    return {
        "x1_pixels": draw_x1_pixels(jax.random.fold_in(arg_keys[4], 71), 0),
        "dout_frames": gaussian_with(arg_keys[1], (CLIPS, F, S, D), 1.0, 6.0, ((0, 16), (1, 16)), (1, 3, 16, 2.0)),
        "w_qkv": scatter_about(arg_keys[2], (D, 3 * D), D ** -0.5, 0.1875),
        "w_out": scatter_about(arg_keys[3], (D, D), D ** -0.5, 0.1875),
    }


EPS = 1e-06

def centre_rows(inputs):
    values = inputs.astype(jnp.float32)
    centred = values - lax.optimization_barrier(jnp.mean(values, axis=-1, keepdims=True))
    inverse = lax.rsqrt(lax.optimization_barrier(jnp.mean(centred * centred, axis=-1, keepdims=True)) + EPS)
    return (centred * inverse, inverse)

def head_scale(values):
    return values * lax.rsqrt(lax.optimization_barrier(jnp.mean(values * values, axis=-1, keepdims=True)) + EPS)

def pair_scale(first, second):
    return (head_scale(first), head_scale(second))

def batched(form, left, right):
    return jnp.einsum(form, left.astype(jnp.float32), right.astype(jnp.float32))

def temporal_terms(inputs, upstream, w_qkv, w_out):
    lead = inputs.shape[:3]
    width = inputs.shape[3]
    tokens_here = lead[0] * lead[1] * lead[2]
    head_size = width // HEADS
    split_shape = lead + (HEADS, head_size)
    standard, inverse = centre_rows(inputs)
    normed = standard.astype(jnp.bfloat16).reshape(tokens_here, width)
    projected = jnp.dot(normed, w_qkv, preferred_element_type=jnp.float32)
    query = projected[:, :width].reshape(split_shape)
    keys_raw = projected[:, width:2 * width].reshape(split_shape)
    values_raw = projected[:, 2 * width:].reshape(split_shape)
    (query_n, keys_n), norm_back = jax.vjp(pair_scale, query, keys_raw)
    query_b = query_n.astype(jnp.bfloat16)
    keys_b = keys_n.astype(jnp.bfloat16)
    values_b = values_raw.astype(jnp.bfloat16)
    factor = head_size ** (-0.5)
    scores = batched('bfphd,bgphd->bphfg', query_b, keys_b) * factor
    weights = jnp.exp(scores)
    probs = weights / lax.optimization_barrier(jnp.sum(weights, axis=-1, keepdims=True))
    probs_b = probs.astype(jnp.bfloat16)
    attended = batched('bphfg,bgphd->bfphd', probs_b, values_b).astype(jnp.bfloat16)
    flat_att = attended.reshape(tokens_here, width)
    flat_up = upstream.reshape(tokens_here, width)
    grad_out = jnp.dot(flat_att.T, flat_up, preferred_element_type=jnp.float32)
    grad_att = jnp.dot(flat_up, w_out.T, preferred_element_type=jnp.float32).astype(jnp.bfloat16).reshape(split_shape)
    grad_probs = batched('bfphd,bgphd->bphfg', grad_att, values_b)
    grad_values = batched('bphfg,bfphd->bgphd', probs_b, grad_att)
    grad_scores = (probs * (grad_probs - lax.optimization_barrier(jnp.sum(probs * grad_probs, axis=-1, keepdims=True))) * factor).astype(jnp.bfloat16)
    grad_qn = batched('bphfg,bgphd->bfphd', grad_scores, keys_b)
    grad_kn = batched('bphfg,bfphd->bgphd', grad_scores, query_b)
    grad_query, grad_keys = norm_back((grad_qn, grad_kn))
    grad_proj = jnp.concatenate([grad_query.reshape(tokens_here, width), grad_keys.reshape(tokens_here, width), grad_values.reshape(tokens_here, width)], axis=1).astype(jnp.bfloat16)
    grad_qkv = jnp.dot(normed.T, grad_proj, preferred_element_type=jnp.float32)
    grad_normed = jnp.dot(grad_proj, w_qkv.T, preferred_element_type=jnp.float32).reshape(lead + (width,))
    branch = inverse * (grad_normed - lax.optimization_barrier(jnp.mean(grad_normed, axis=-1, keepdims=True)) - standard * lax.optimization_barrier(jnp.mean(grad_normed * standard, axis=-1, keepdims=True)))
    return (branch.astype(jnp.bfloat16), grad_qkv, grad_out)

def reference(x1_pixels, dout_frames, w_qkv, w_out):

    def per_clip(carry, pair):
        inputs, upstream = pair
        branch, grad_qkv, grad_out = temporal_terms(inputs[None], upstream[None], w_qkv, w_out)
        return ((carry[0] + grad_qkv, carry[1] + grad_out), branch[0])
    start = (jnp.zeros((D, 3 * D), jnp.float32), jnp.zeros((D, D), jnp.float32))
    (grad_qkv, grad_out), branches = lax.scan(per_clip, start, (x1_pixels, dout_frames))
    factor = 1.0 / math.sqrt(CLIPS * F * S)
    d_x1 = (dout_frames.astype(jnp.float32) + branches.astype(jnp.float32)).astype(jnp.bfloat16)
    return (d_x1, grad_qkv * factor, grad_out * factor)
```

```python
import functools

import jax
import jax.numpy as jnp
from jax import lax
from jax.experimental import pallas as pl
from jax.experimental.pallas import tpu as pltpu
from jax.sharding import PartitionSpec as P

F32, BF16 = jnp.float32, jnp.bfloat16
EPS = 1e-06
HEADS = 16
HD = 72
D = 1152
FR = 16
PX = 16
TOK = FR * PX
FACTOR = HD**-0.5
NT = (((1,), (1,)), ((), ()))
TN = (((0,), (0,)), ((), ()))
ROWS_A, ROWS_B = 80, 64
MIB = 1 << 20


def dot(a, b, dims=None):
    if dims is None:
        return jnp.dot(a, b, preferred_element_type=F32)
    return lax.dot_general(a, b, dims, preferred_element_type=F32)


def seq_peer(offset):
    return {"seq": lax.rem(lax.axis_index("seq") + offset, 16)}


def place():
    dp, seq = lax.axis_index("dp"), lax.axis_index("seq")
    return dp // 4, (dp // 2) % 2, dp % 2, seq // 4, seq % 4


def spread_kernel(dout_ref, up_ref, send_sems, recv_sems, own_sem):
    me = lax.axis_index("seq")
    barrier = pltpu.get_barrier_semaphore()
    for o in range(1, 16):
        pl.semaphore_signal(barrier, inc=1, device_id=seq_peer(o))
    pl.semaphore_wait(barrier, 15)

    def piece(o):
        return pltpu.make_async_remote_copy(
            src_ref=dout_ref.at[lax.rem(me + o, 16)],
            dst_ref=up_ref.at[me],
            send_sem=send_sems.at[o],
            recv_sem=recv_sems.at[o],
            device_id=seq_peer(o),
        )

    own = pltpu.make_async_copy(dout_ref.at[me], up_ref.at[me], own_sem)
    own.start()
    for o in range(1, 16):
        piece(o).start()
    own.wait()
    for o in range(1, 16):
        piece(o).wait()


def spread(dout):
    return pl.pallas_call(
        spread_kernel,
        out_shape=jax.ShapeDtypeStruct((16, PX, D), BF16),
        in_specs=[pl.BlockSpec(memory_space=pltpu.VMEM)],
        out_specs=pl.BlockSpec(memory_space=pltpu.VMEM),
        scratch_shapes=[
            pltpu.SemaphoreType.DMA((16,)),
            pltpu.SemaphoreType.DMA((16,)),
            pltpu.SemaphoreType.DMA,
        ],
        compiler_params=pltpu.CompilerParams(collective_id=1, has_side_effects=True),
    )(dout)


def to_rows(block):
    return jnp.concatenate([block[:, 8 * p : 8 * p + 8, :].reshape(128, D) for p in range(2)], axis=0)


def from_rows(rows):
    return jnp.concatenate([rows[128 * p : 128 * p + 128].reshape(FR, 8, D) for p in range(2)], axis=1)


def attend(q, k, v, ga, mask):
    rq = lax.rsqrt(jnp.sum(q * q, axis=0, keepdims=True) * (1.0 / HD) + EPS)
    rk = lax.rsqrt(jnp.sum(k * k, axis=0, keepdims=True) * (1.0 / HD) + EPS)
    qn, kn = (q * rq).astype(BF16), (k * rk).astype(BF16)
    vb, gb = v.astype(BF16), ga.astype(BF16)
    out = []
    for p in range(2):
        at = slice(128 * p, 128 * p + 128)
        qh, kh, vh, gh = qn[:, at], kn[:, at], vb[:, at], gb[:, at]
        e = jnp.exp(dot(kh, qh, TN) * FACTOR).reshape(FR, 8, 128)
        probs = e * (mask / jnp.sum(e, axis=0))[None]
        pb = probs.reshape(128, 128).astype(BF16)
        att = dot(vh, pb)
        grad_probs = dot(vh, gh, TN).reshape(FR, 8, 128)
        total = jnp.sum(probs * grad_probs, axis=0)
        gs = (probs * (grad_probs - total[None]) * FACTOR).reshape(128, 128).astype(BF16)
        gv = dot(gh, pb, NT)
        gqn = dot(kh, gs)
        gkn = dot(qh, gs, NT)
        out.append((att, gqn, gkn, gv))
    att, gqn, gkn, gv = (jnp.concatenate(pair, axis=1) for pair in zip(*out))
    tq = jnp.sum(gqn * q, axis=0, keepdims=True) * (1.0 / HD)
    tk = jnp.sum(gkn * k, axis=0, keepdims=True) * (1.0 / HD)
    gq = rq * gqn - q * (rq * rq * rq * tq)
    gk = rk * gkn - k * (rk * rk * rk * tk)
    return att, gq, gk, gv


def local_kernel(x_ref, up_ref, wqkv_ref, wout_ref, branch_ref, nt_ref, at_ref, gp_ref, ut_ref, std, proj, gat):
    x = to_rows(x_ref[...].astype(F32))
    centred = x - jnp.mean(x, axis=-1, keepdims=True)
    inverse = lax.rsqrt(jnp.mean(centred * centred, axis=-1, keepdims=True) + EPS)
    standard = centred * inverse
    std[...] = standard
    normed = standard.astype(BF16)
    standard_t = standard.T
    for c in range(2):
        nt_ref[c] = jnp.concatenate(
            [standard_t[HD * (2 * b + c) : HD * (2 * b + c + 1)] for b in range(8)], axis=0
        ).astype(BF16)
    for t in range(3):
        proj[D * t : D * t + D, :] = dot(normed, wqkv_ref[:, D * t : D * t + D]).T
    ut = to_rows(up_ref[...].astype(F32)).T.astype(BF16)
    ut_ref[0:96, :] = jnp.zeros((96, TOK), BF16)
    ut_ref[96 : 96 + D, :] = ut
    gat[...] = dot(wout_ref[...], ut)
    gp_ref[3 * D : 3 * D + 32, :] = jnp.zeros((32, TOK), BF16)
    mask = (
        lax.broadcasted_iota(jnp.int32, (8, 128), 0) == lax.broadcasted_iota(jnp.int32, (8, 128), 1) % 8
    ).astype(F32)

    def group(i, carry):
        base = pl.multiple_of(i * 288, 288)
        blocks = [proj[pl.ds(pl.multiple_of(D * t + base, 288), 288), :] for t in range(3)]
        blocks.append(gat[pl.ds(base, 288), :])
        heads = [attend(*(b[HD * h : HD * h + HD] for b in blocks), mask) for h in range(4)]
        half = pl.multiple_of(i * 144, 144)
        for c in range(2):
            at_ref[c, pl.ds(half, 144), :] = jnp.concatenate([heads[c][0], heads[c + 2][0]], axis=0).astype(BF16)
        for t in range(3):
            gp_ref[pl.ds(pl.multiple_of(D * t + base, 288), 288), :] = jnp.concatenate(
                [h[1 + t] for h in heads], axis=0
            ).astype(BF16)
        return carry

    lax.fori_loop(0, 4, group, 0)
    gn = dot(wqkv_ref[...], gp_ref[0 : 3 * D, :]).T
    standard = std[...]
    branch = inverse * (
        gn
        - jnp.mean(gn, axis=-1, keepdims=True)
        - standard * jnp.mean(gn * standard, axis=-1, keepdims=True)
    )
    branch_ref[...] = from_rows(branch).astype(BF16)


def local_math(x, up, wqkv, wout):
    vmem = pl.BlockSpec(memory_space=pltpu.VMEM)
    return pl.pallas_call(
        local_kernel,
        out_shape=[
            jax.ShapeDtypeStruct((FR, PX, D), BF16),
            jax.ShapeDtypeStruct((2, D // 2, TOK), BF16),
            jax.ShapeDtypeStruct((2, D // 2, TOK), BF16),
            jax.ShapeDtypeStruct((3 * D + 32, TOK), BF16),
            jax.ShapeDtypeStruct((D + 96, TOK), BF16),
        ],
        in_specs=[vmem] * 4,
        out_specs=[vmem] * 5,
        scratch_shapes=[
            pltpu.VMEM((TOK, D), F32),
            pltpu.VMEM((3 * D, TOK), F32),
            pltpu.VMEM((D, TOK), F32),
        ],
        compiler_params=pltpu.CompilerParams(vmem_limit_bytes=48 * MIB),
    )(x, up, wqkv, wout)


def reduce_kernel(
    nt, at, gp, ut, branch, dout, d_x1, g_qkv, g_out,
    pn, pa, pg, pu, s1, s2, r1, r2, t1, t2, u1, u2, total, zs, zr, kept, hs, hr, back,
    pair_s, pair_r, back_s, back_r, x_s, x_r, y_s, y_r, x2_s, x2_r, y2_s, y2_r, zl_s, zl_r, zh_s, zh_r,
):
    dp, seq = lax.axis_index("dp"), lax.axis_index("seq")
    y, zl, core, x, zh = place()

    def x_peer(o):
        return {"seq": lax.rem(x + o, 4) * 4 + zh}

    def zh_peer(o):
        return {"seq": x * 4 + lax.rem(zh + o, 4)}

    def y_peer(o):
        return {"dp": lax.rem(y + o, 4) * 4 + zl * 2 + core}

    core_peer = {"dp": dp + 1 - 2 * core}
    zl_peer = {"dp": dp + 2 - 4 * zl}
    barrier = pltpu.get_barrier_semaphore()
    for peer in [seq_peer(o) for o in range(1, 16)] + [y_peer(o) for o in range(1, 4)] + [core_peer, zl_peer]:
        pl.semaphore_signal(barrier, inc=1, device_id=peer)
    pl.semaphore_wait(barrier, 20)

    def send(src, dst, s_sem, r_sem, peer):
        copy = pltpu.make_async_remote_copy(src_ref=src, dst_ref=dst, send_sem=s_sem, recv_sem=r_sem, device_id=peer)
        return copy

    pair = [
        send(nt.at[1 - core], pn, pair_s.at[0], pair_r.at[0], core_peer),
        send(gp, pg, pair_s.at[1], pair_r.at[1], core_peer),
        send(at.at[1 - core], pa, pair_s.at[2], pair_r.at[2], core_peer),
        send(ut, pu, pair_s.at[3], pair_r.at[3], core_peer),
    ]
    for copy in pair:
        copy.start()
    returns = [
        send(branch.at[lax.rem(seq + o, 16)], back.at[seq], back_s.at[o], back_r.at[o], seq_peer(o))
        for o in range(1, 16)
    ]
    for copy in returns:
        copy.start()
    for copy in pair:
        copy.wait()

    lane = lax.broadcasted_iota(jnp.int32, (D // 2, 128), 1)
    first, second = [], []
    for step, o in enumerate((2, 1, 3, 0)):
        xd = lax.rem(x + o, 4)
        q_rows = pl.ds(pl.multiple_of(xd * 864, 16), 896)
        o_rows = pl.ds(pl.multiple_of(xd * 288, 16), 384)
        left = dot(nt[core], gp[q_rows, :], NT) + dot(pn[...], pg[q_rows, :], NT)
        right = dot(at[core], ut[o_rows, :], NT) + dot(pa[...], pu[o_rows, :], NT)
        middle = jnp.where(lane < 96, left[:, 768:896], right[:, 0:128])
        for cols, val in ((slice(0, 768), left[:, 0:768]), (slice(768, 896), middle), (slice(896, D), right[:, 128:384])):
            val = val.astype(BF16)
            for b in range(4):
                s1[xd, b, :, cols] = val[144 * b : 144 * b + ROWS_A]
                s2[b, xd, :, cols] = val[144 * b + ROWS_A : 144 * b + 144]
        if o:
            copy = send(s1.at[xd], r1.at[o - 1], x_s.at[o - 1], x_r.at[o - 1], x_peer(o))
            copy.start()
            first.append(copy)
        for oy in (2, 1, 3):
            yd = lax.rem(y + oy, 4)
            copy = send(
                s2.at[yd, xd], r2.at[oy - 1, xd], y_s.at[step * 3 + oy - 1], y_r.at[step * 3 + oy - 1], y_peer(oy)
            )
            copy.start()
            second.append(copy)

    for copy in first:
        copy.wait()
    for copy in second:
        copy.wait()

    def add(own, *others):
        value = own.astype(F32)
        for other in others:
            value = value + other.astype(F32)
        return value

    later = []
    for o in (2, 1, 3, 0):
        yd, xd = lax.rem(y + o, 4), lax.rem(x + o, 4)
        t1[yd] = add(s1[x, yd], r1[0, yd], r1[1, yd], r1[2, yd]).astype(BF16)
        t2[xd] = add(s2[y, xd], r2[0, xd], r2[1, xd], r2[2, xd]).astype(BF16)
        if o:
            later.append(send(t1.at[yd], u1.at[o - 1], y2_s.at[o - 1], y2_r.at[o - 1], y_peer(o)))
            later[-1].start()
            later.append(send(t2.at[xd], u2.at[o - 1], x2_s.at[o - 1], x2_r.at[o - 1], x_peer(o)))
            later[-1].start()
    for copy in later:
        copy.wait()
    total[0:ROWS_A, :] = add(t1[y], u1[0], u1[1], u1[2])
    total[ROWS_A:144, :] = add(t2[x], u2[0], u2[1], u2[2])

    zs[...] = total[pl.ds(pl.multiple_of(64 * (1 - zl), 64), 80), :].astype(BF16)
    copy = send(zs, zr, zl_s, zl_r, zl_peer)
    copy.start()
    for copy_back in returns:
        copy_back.wait()
    back[seq] = branch[seq]
    d_x1[...] = (dout[...].astype(F32) + back[...].astype(F32)).astype(BF16)
    copy.wait()
    kept[...] = total[pl.ds(pl.multiple_of(64 * zl, 64), 80), :] + zr[...].astype(F32)
    value = kept[pl.ds(pl.multiple_of(8 * zl, 8), 72), :]
    hs[...] = jnp.zeros_like(hs)
    for b in range(4):
        hs[b, 0:72, 0:216] = value[:, 216 * b : 216 * b + 216].astype(BF16)
        hs[b, 0:72, 256:328] = value[:, 864 + 72 * b : 936 + 72 * b].astype(BF16)
    ends = [
        send(hs.at[lax.rem(zh + o, 4)], hr.at[o - 1], zh_s.at[o - 1], zh_r.at[o - 1], zh_peer(o)) for o in (2, 1, 3)
    ]
    for copy in ends:
        copy.start()
    for copy in ends:
        copy.wait()
    result = add(hs[zh], hr[0], hr[1], hr[2]) * (1.0 / 256.0)
    g_qkv[...] = result[0:72, 0:216]
    g_out[...] = result[0:72, 256:328]


def reduce_all(nt, at, gp, ut, branch, dout):
    vmem = pl.BlockSpec(memory_space=pltpu.VMEM)
    half = D // 2
    dma = pltpu.SemaphoreType.DMA
    return pl.pallas_call(
        reduce_kernel,
        out_shape=[
            jax.ShapeDtypeStruct((16, PX, D), BF16),
            jax.ShapeDtypeStruct((72, 216), F32),
            jax.ShapeDtypeStruct((72, 72), F32),
        ],
        in_specs=[vmem] * 6,
        out_specs=[vmem] * 3,
        scratch_shapes=[
            pltpu.VMEM((half, TOK), BF16),
            pltpu.VMEM((half, TOK), BF16),
            pltpu.VMEM((3 * D + 32, TOK), BF16),
            pltpu.VMEM((D + 96, TOK), BF16),
            pltpu.VMEM((4, 4, ROWS_A, D), BF16),
            pltpu.VMEM((4, 4, ROWS_B, D), BF16),
            pltpu.VMEM((3, 4, ROWS_A, D), BF16),
            pltpu.VMEM((3, 4, ROWS_B, D), BF16),
            pltpu.VMEM((4, ROWS_A, D), BF16),
            pltpu.VMEM((4, ROWS_B, D), BF16),
            pltpu.VMEM((3, ROWS_A, D), BF16),
            pltpu.VMEM((3, ROWS_B, D), BF16),
            pltpu.VMEM((144, D), F32),
            pltpu.VMEM((80, D), BF16),
            pltpu.VMEM((80, D), BF16),
            pltpu.VMEM((80, D), F32),
            pltpu.VMEM((4, 80, 384), BF16),
            pltpu.VMEM((3, 80, 384), BF16),
            pltpu.VMEM((16, PX, D), BF16),
            dma((4,)), dma((4,)),
            dma((16,)), dma((16,)),
            dma((3,)), dma((3,)),
            dma((12,)), dma((12,)),
            dma((3,)), dma((3,)),
            dma((3,)), dma((3,)),
            dma, dma,
            dma((3,)), dma((3,)),
        ],
        compiler_params=pltpu.CompilerParams(
            collective_id=2, has_side_effects=True, vmem_limit_bytes=48 * MIB
        ),
    )(nt, at, gp, ut, branch, dout)


def local(x1_pixels, dout_frames, w_qkv, w_out):
    x = x1_pixels.reshape(FR, PX, D)
    dout = dout_frames.reshape(16, PX, D)
    up = spread(dout)
    branch, nt, at, gp, ut = local_math(x, up, w_qkv, w_out)
    d_x1, g_qkv, g_out = reduce_all(nt, at, gp, ut, branch, dout)
    return d_x1.reshape(dout_frames.shape), g_qkv, g_out


def solution(mesh):
    return jax.shard_map(
        local,
        mesh=mesh,
        in_specs=(P("dp", None, "seq", None), P("dp", "seq", None, None), P(), P()),
        out_specs=(P("dp", "seq", None, None), P("dp", "seq"), P("dp", "seq")),
        check_vma=False,
    )
```

```python
import jax
import jax.numpy as jnp
from jax import lax
from jax.experimental import pallas as pl
from jax.experimental.pallas import tpu as pltpu
from jax.sharding import PartitionSpec as P

F32, BF16 = jnp.float32, jnp.bfloat16
EPS = 1e-06
HD = 72
D = 1152
HALF = D // 2
FR = 16
PX = 16
TOK = FR * PX
FACTOR = HD**-0.5
NT = (((1,), (1,)), ((), ()))
TN = (((0,), (0,)), ((), ()))
ROWS_A, ROWS_B = 64, 80
QW, OW = 896, 384
MIB = 1 << 20


def dot(a, b, dims=None):
    if dims is None:
        return jnp.dot(a, b, preferred_element_type=F32)
    return lax.dot_general(a, b, dims, preferred_element_type=F32)


def to_rows(block):
    return jnp.concatenate([block[:, 8 * p : 8 * p + 8, :].reshape(128, D) for p in range(2)], axis=0)


def from_rows(rows):
    return jnp.concatenate([rows[128 * p : 128 * p + 128].reshape(FR, 8, D) for p in range(2)], axis=1)


def head_scale(v):
    return lax.rsqrt(jnp.sum(v * v, axis=0, keepdims=True) * (1.0 / HD) + EPS)


def forward_head(q, k, v, mask, keep):
    qn, kn, vb = (q * head_scale(q)).astype(BF16), (k * head_scale(k)).astype(BF16), v.astype(BF16)
    out = []
    for p in range(2):
        at = slice(128 * p, 128 * p + 128)
        e = jnp.exp(dot(kn[:, at], qn[:, at], TN) * FACTOR).reshape(FR, 8, 128)
        probs = (e * (mask / jnp.sum(e, axis=0))[None]).reshape(128, 128)
        keep(p, probs)
        out.append(dot(vb[:, at], probs.astype(BF16)))
    return jnp.concatenate(out, axis=1)


def backward_head(q, k, v, ga, probs_of):
    rq, rk = head_scale(q), head_scale(k)
    qn, kn = (q * rq).astype(BF16), (k * rk).astype(BF16)
    vb, gb = v.astype(BF16), ga.astype(BF16)
    out = []
    for p in range(2):
        at = slice(128 * p, 128 * p + 128)
        qh, kh, vh, gh = qn[:, at], kn[:, at], vb[:, at], gb[:, at]
        flat = probs_of(p)
        probs = flat.reshape(FR, 8, 128)
        pb = flat.astype(BF16)
        grad_probs = dot(vh, gh, TN).reshape(FR, 8, 128)
        total = jnp.sum(probs * grad_probs, axis=0)
        gs = (probs * (grad_probs - total[None]) * FACTOR).reshape(128, 128).astype(BF16)
        out.append((dot(kh, gs), dot(qh, gs, NT), dot(gh, pb, NT)))
    gqn, gkn, gv = (jnp.concatenate(pair, axis=1) for pair in zip(*out))
    tq = jnp.sum(gqn * q, axis=0, keepdims=True) * (1.0 / HD)
    tk = jnp.sum(gkn * k, axis=0, keepdims=True) * (1.0 / HD)
    gq = rq * gqn - q * (rq * rq * rq * tq)
    gk = rk * gkn - k * (rk * rk * rk * tk)
    return gq, gk, gv


def add(own, *others):
    value = own.astype(F32)
    for other in others:
        value = value + other.astype(F32)
    return value


def kernel(
    x_hbm, dout_hbm, wqkv_hbm, wout_hbm, back_ref, res_ref,
    xv, wqkv, wout, up, std, proj, gat, probs, branch, nt, at, gp, ut, pn, pa, pg, pu,
    s1, s2, so, r1, r2, ro, t1, t2, to, u1, u2, uo, total, zs, zr, kept, hs, hr,
    load, sp_s, sp_r, pair_s, pair_r, bk_s, bk_r, x_s, x_r, y_s, y_r, o_s, o_r,
    x2_s, x2_r, y2_s, y2_r, zl_s, zl_r, zh_s, zh_r,
):
    dp, seq = lax.axis_index("dp"), lax.axis_index("seq")
    y, zl, core, x, zh = dp // 4, (dp // 2) % 2, dp % 2, seq // 4, seq % 4

    def seq_peer(o):
        return {"seq": lax.rem(seq + o, 16)}

    def x_peer(o):
        return {"seq": lax.rem(x + o, 4) * 4 + zh}

    def zh_peer(o):
        return {"seq": x * 4 + lax.rem(zh + o, 4)}

    def y_peer(o):
        return {"dp": lax.rem(y + o, 4) * 4 + zl * 2 + core}

    core_peer = {"dp": dp + 1 - 2 * core}
    zl_peer = {"dp": dp + 2 - 4 * zl}

    def send(src, dst, s_sem, r_sem, peer):
        copy = pltpu.make_async_remote_copy(src_ref=src, dst_ref=dst, send_sem=s_sem, recv_sem=r_sem, device_id=peer)
        copy.start()
        return copy

    def wait(copies):
        for copy in copies:
            copy.wait()

    barrier = pltpu.get_barrier_semaphore()
    for peer in [seq_peer(o) for o in range(1, 16)] + [y_peer(o) for o in range(1, 4)] + [core_peer, zl_peer]:
        pl.semaphore_signal(barrier, inc=1, device_id=peer)
    loads = [
        pltpu.make_async_copy(x_hbm, xv, load.at[0]),
        pltpu.make_async_copy(wqkv_hbm, wqkv, load.at[1]),
        pltpu.make_async_copy(wout_hbm, wout, load.at[2]),
        pltpu.make_async_copy(dout_hbm.at[seq], up.at[seq], load.at[3]),
    ]
    for copy in loads:
        copy.start()
    pl.semaphore_wait(barrier, 20)
    order = (8, 7, 9, 6, 10, 5, 11, 4, 12, 3, 13, 2, 14, 1, 15)
    spread = [
        send(dout_hbm.at[lax.rem(seq + o, 16)], up.at[seq], sp_s.at[o], sp_r.at[o], seq_peer(o)) for o in order
    ]

    loads[0].wait()
    rows = to_rows(xv[...].astype(F32))
    centred = rows - jnp.mean(rows, axis=-1, keepdims=True)
    inverse = lax.rsqrt(jnp.mean(centred * centred, axis=-1, keepdims=True) + EPS)
    standard = centred * inverse
    std[...] = standard
    normed = standard.astype(BF16)
    standard_t = standard.T
    for c in range(2):
        nt[c] = jnp.concatenate(
            [standard_t[HD * (2 * b + c) : HD * (2 * b + c + 1)] for b in range(8)], axis=0
        ).astype(BF16)
    pair_n = send(nt.at[1 - core], pn, pair_s.at[12], pair_r.at[12], core_peer)
    loads[1].wait()
    for t in range(3):
        proj[D * t : D * t + D, :] = dot(normed, wqkv[:, D * t : D * t + D]).T

    mask = (
        lax.broadcasted_iota(jnp.int32, (8, 128), 0) == lax.broadcasted_iota(jnp.int32, (8, 128), 1) % 8
    ).astype(F32)

    def forward_group(i, carry):
        base = pl.multiple_of(i * 288, 288)
        blocks = [proj[pl.ds(pl.multiple_of(D * t + base, 288), 288), :] for t in range(3)]
        heads = []
        for h in range(4):

            def keep(p, value, h=h):
                probs[i * 4 + h, p] = value

            heads.append(forward_head(*(b[HD * h : HD * h + HD] for b in blocks), mask, keep))
        half = pl.multiple_of(i * 144, 144)
        for c in range(2):
            at[c, pl.ds(half, 144), :] = jnp.concatenate([heads[c], heads[c + 2]], axis=0).astype(BF16)
        return carry

    lax.fori_loop(0, 4, forward_group, 0)
    pair_a = send(at.at[1 - core], pa, pair_s.at[13], pair_r.at[13], core_peer)

    loads[2].wait()
    loads[3].wait()
    wait(spread)
    up_t = to_rows(up[...].astype(F32)).T.astype(BF16)
    ut[...] = up_t
    pair_u = send(ut, pu, pair_s.at[14], pair_r.at[14], core_peer)
    gat[...] = dot(wout[...], up_t)
    wait([pair_n, pair_a, pair_u])

    own_a = at[core]
    for n in range(3):
        cols = slice(OW * n, OW * n + OW)
        val = (dot(own_a, ut[cols, :], NT) + dot(pa[...], pu[cols, :], NT)).astype(BF16)
        for b in range(4):
            so[b, :, cols] = val[144 * b : 144 * b + 144]
    out_y = []
    for o in (2, 1, 3):
        out_y.append(send(so.at[lax.rem(y + o, 4)], ro.at[o - 1], o_s.at[o - 1], o_r.at[o - 1], y_peer(o)))

    gp[3 * D : 3 * D + 32, :] = jnp.zeros((32, TOK), BF16)
    pg[3 * D : 3 * D + 32, :] = jnp.zeros((32, TOK), BF16)

    def gp_copy(i, t):
        span = pl.ds(pl.multiple_of(D * t + i * 288, 288), 288)
        return pltpu.make_async_remote_copy(
            src_ref=gp.at[span], dst_ref=pg.at[span],
            send_sem=pair_s.at[3 * i + t], recv_sem=pair_r.at[3 * i + t], device_id=core_peer,
        )

    def backward_group(i, carry):
        base = pl.multiple_of(i * 288, 288)
        blocks = [proj[pl.ds(pl.multiple_of(D * t + base, 288), 288), :] for t in range(3)]
        blocks.append(gat[pl.ds(base, 288), :])
        heads = [
            backward_head(*(b[HD * h : HD * h + HD] for b in blocks), lambda p, h=h: probs[i * 4 + h, p])
            for h in range(4)
        ]
        for t in range(3):
            gp[pl.ds(pl.multiple_of(D * t + base, 288), 288), :] = jnp.concatenate(
                [h[t] for h in heads], axis=0
            ).astype(BF16)
            gp_copy(i, t).start()
        return carry

    lax.fori_loop(0, 4, backward_group, 0)
    wait([gp_copy(i, t) for i in range(4) for t in range(3)])

    own_n = nt[core]
    first, second = [], []
    for step, o in enumerate((2, 1, 3, 0)):
        xd = lax.rem(x + o, 4)
        span = pl.ds(pl.multiple_of(xd * 864, 16), QW)
        val = (dot(own_n, gp[span, :], NT) + dot(pn[...], pg[span, :], NT)).astype(BF16)
        for b in range(4):
            s1[xd, b] = val[144 * b : 144 * b + ROWS_A]
            s2[b, xd] = val[144 * b + ROWS_A : 144 * b + 144]
        if o:
            first.append(send(s1.at[xd], r1.at[o - 1], x_s.at[o - 1], x_r.at[o - 1], x_peer(o)))
        for oy in (2, 1, 3):
            sem = step * 3 + oy - 1
            second.append(
                send(s2.at[lax.rem(y + oy, 4), xd], r2.at[oy - 1, xd], y_s.at[sem], y_r.at[sem], y_peer(oy))
            )

    gn = dot(wqkv[...], gp[0 : 3 * D, :]).T
    standard = std[...]
    value = inverse * (
        gn
        - jnp.mean(gn, axis=-1, keepdims=True)
        - standard * jnp.mean(gn * standard, axis=-1, keepdims=True)
    )
    branch[...] = from_rows(value).astype(BF16)
    returns = [
        send(branch.at[lax.rem(seq + o, 16)], back_ref.at[seq], bk_s.at[o], bk_r.at[o], seq_peer(o)) for o in order
    ]
    back_ref[seq] = branch[seq]

    wait(out_y)
    val = add(so[y], ro[0], ro[1], ro[2]).astype(BF16)
    for b in range(4):
        to[b, :, 0:288] = val[:, 288 * b : 288 * b + 288]
        to[b, :, 288:OW] = jnp.zeros((144, OW - 288), BF16)
    later = [
        send(to.at[lax.rem(x + o, 4)], uo.at[o - 1], x2_s.at[o + 2], x2_r.at[o + 2], x_peer(o)) for o in (2, 1, 3)
    ]
    wait(first)
    for o in (2, 1, 3, 0):
        yd = lax.rem(y + o, 4)
        t1[yd] = add(s1[x, yd], r1[0, yd], r1[1, yd], r1[2, yd]).astype(BF16)
        if o:
            later.append(send(t1.at[yd], u1.at[o - 1], y2_s.at[o - 1], y2_r.at[o - 1], y_peer(o)))
    wait(second)
    for o in (2, 1, 3, 0):
        xd = lax.rem(x + o, 4)
        t2[xd] = add(s2[y, xd], r2[0, xd], r2[1, xd], r2[2, xd]).astype(BF16)
        if o:
            later.append(send(t2.at[xd], u2.at[o - 1], x2_s.at[o - 1], x2_r.at[o - 1], x_peer(o)))
    wait(later)
    total[0:ROWS_A, 0:QW] = add(t1[y], u1[0], u1[1], u1[2])
    total[ROWS_A:144, 0:QW] = add(t2[x], u2[0], u2[1], u2[2])
    total[:, QW:] = add(to[x], uo[0], uo[1], uo[2])

    zs[...] = total[pl.ds(pl.multiple_of(64 * (1 - zl), 64), 80), :].astype(BF16)
    send(zs, zr, zl_s, zl_r, zl_peer).wait()
    kept[...] = total[pl.ds(pl.multiple_of(64 * zl, 64), 80), :] + zr[...].astype(F32)
    value = kept[pl.ds(pl.multiple_of(8 * zl, 8), 72), :]

    hs[...] = jnp.zeros_like(hs)
    for b in range(4):
        hs[b, 0:72, 0:216] = value[:, 216 * b : 216 * b + 216].astype(BF16)
        hs[b, 0:72, 256:328] = value[:, QW + 72 * b : QW + 72 * b + 72].astype(BF16)
    wait(
        [
            send(hs.at[lax.rem(zh + o, 4)], hr.at[o - 1], zh_s.at[o - 1], zh_r.at[o - 1], zh_peer(o))
            for o in (2, 1, 3)
        ]
    )
    res_ref[...] = add(hs[zh], hr[0], hr[1], hr[2])
    wait(returns)


def fused(x, dout, wqkv, wout):
    dma = pltpu.SemaphoreType.DMA

    def buf(*shape, dtype=BF16):
        return pltpu.VMEM(shape, dtype)

    return pl.pallas_call(
        kernel,
        out_shape=[jax.ShapeDtypeStruct((16, PX, D), BF16), jax.ShapeDtypeStruct((80, OW), F32)],
        in_specs=[pl.BlockSpec(memory_space=pl.ANY)] * 4,
        out_specs=[pl.BlockSpec(memory_space=pltpu.VMEM)] * 2,
        scratch_shapes=[
            buf(FR, PX, D), buf(D, 3 * D), buf(D, D), buf(16, PX, D),
            buf(TOK, D, dtype=F32), buf(3 * D, TOK, dtype=F32), buf(D, TOK, dtype=F32),
            buf(16, 2, 128, 128, dtype=F32), buf(FR, PX, D),
            buf(2, HALF, TOK), buf(2, HALF, TOK), buf(3 * D + 32, TOK), buf(D, TOK),
            buf(HALF, TOK), buf(HALF, TOK), buf(3 * D + 32, TOK), buf(D, TOK),
            buf(4, 4, ROWS_A, QW), buf(4, 4, ROWS_B, QW), buf(4, 144, D),
            buf(3, 4, ROWS_A, QW), buf(3, 4, ROWS_B, QW), buf(3, 144, D),
            buf(4, ROWS_A, QW), buf(4, ROWS_B, QW), buf(4, 144, OW),
            buf(3, ROWS_A, QW), buf(3, ROWS_B, QW), buf(3, 144, OW),
            buf(144, QW + OW, dtype=F32), buf(80, QW + OW), buf(80, QW + OW),
            buf(80, QW + OW, dtype=F32), buf(4, 80, OW), buf(3, 80, OW),
            dma((4,)), dma((16,)), dma((16,)), dma((15,)), dma((15,)), dma((16,)), dma((16,)),
            dma((3,)), dma((3,)), dma((12,)), dma((12,)), dma((3,)), dma((3,)),
            dma((6,)), dma((6,)), dma((3,)), dma((3,)), dma, dma, dma((3,)), dma((3,)),
        ],
        compiler_params=pltpu.CompilerParams(
            collective_id=1, has_side_effects=True, vmem_limit_bytes=56 * MIB
        ),
    )(x, dout, wqkv, wout)


def local(x1_pixels, dout_frames, w_qkv, w_out):
    x = x1_pixels.reshape(FR, PX, D)
    dout = dout_frames.reshape(16, PX, D)
    back, res = fused(x, dout, w_qkv, w_out)
    d_x1 = (dout.astype(F32) + back.astype(F32)).astype(BF16).reshape(dout_frames.shape)
    res = res * (1.0 / 256.0)
    return d_x1, res[0:72, 0:216], res[0:72, 256:328]


def solution(mesh):
    return jax.shard_map(
        local,
        mesh=mesh,
        in_specs=(P("dp", None, "seq", None), P("dp", "seq", None, None), P(), P()),
        out_specs=(P("dp", "seq", None, None), P("dp", "seq"), P("dp", "seq")),
        check_vma=False,
    )
```

```python
import jax
import jax.numpy as jnp
from jax import lax
from jax.experimental import pallas as pl
from jax.experimental.pallas import tpu as pltpu
from jax.sharding import PartitionSpec as P

F32, BF16 = jnp.float32, jnp.bfloat16
EPS = 1e-06
HD = 72
D = 1152
HALF = D // 2
FR = 16
PX = 16
TOK = FR * PX
FACTOR = HD**-0.5
NT = (((1,), (1,)), ((), ()))
TN = (((0,), (0,)), ((), ()))
QW, OW = 896, 384
MIB = 1 << 20


def dot(a, b, dims=None):
    if dims is None:
        return jnp.dot(a, b, preferred_element_type=F32)
    return lax.dot_general(a, b, dims, preferred_element_type=F32)


def to_rows(block):
    return jnp.concatenate([block[:, 8 * p : 8 * p + 8, :].reshape(128, D) for p in range(2)], axis=0)


def from_rows(rows):
    return jnp.concatenate([rows[128 * p : 128 * p + 128].reshape(FR, 8, D) for p in range(2)], axis=1)


def head_scale(v):
    return lax.rsqrt(jnp.sum(v * v, axis=0, keepdims=True) * (1.0 / HD) + EPS)


def forward_head(q, k, v, mask, keep):
    qn, kn, vb = (q * head_scale(q)).astype(BF16), (k * head_scale(k)).astype(BF16), v.astype(BF16)
    out = []
    for p in range(2):
        at = slice(128 * p, 128 * p + 128)
        e = jnp.exp(dot(kn[:, at], qn[:, at], TN) * FACTOR).reshape(FR, 8, 128)
        probs = (e * (mask / jnp.sum(e, axis=0))[None]).reshape(128, 128)
        keep(p, probs)
        out.append(dot(vb[:, at], probs.astype(BF16)))
    return jnp.concatenate(out, axis=1)


def backward_head(q, k, v, ga, probs_of):
    rq, rk = head_scale(q), head_scale(k)
    qn, kn = (q * rq).astype(BF16), (k * rk).astype(BF16)
    vb, gb = v.astype(BF16), ga.astype(BF16)
    out = []
    for p in range(2):
        at = slice(128 * p, 128 * p + 128)
        qh, kh, vh, gh = qn[:, at], kn[:, at], vb[:, at], gb[:, at]
        flat = probs_of(p)
        probs = flat.reshape(FR, 8, 128)
        pb = flat.astype(BF16)
        grad_probs = dot(vh, gh, TN).reshape(FR, 8, 128)
        total = jnp.sum(probs * grad_probs, axis=0)
        gs = (probs * (grad_probs - total[None]) * FACTOR).reshape(128, 128).astype(BF16)
        out.append((dot(kh, gs), dot(qh, gs, NT), dot(gh, pb, NT)))
    gqn, gkn, gv = (jnp.concatenate(pair, axis=1) for pair in zip(*out))
    tq = jnp.sum(gqn * q, axis=0, keepdims=True) * (1.0 / HD)
    tk = jnp.sum(gkn * k, axis=0, keepdims=True) * (1.0 / HD)
    gq = rq * gqn - q * (rq * rq * rq * tq)
    gk = rk * gkn - k * (rk * rk * rk * tk)
    return gq, gk, gv


def add(own, *others):
    value = own.astype(F32)
    for other in others:
        value = value + other.astype(F32)
    return value


def kernel(
    x_hbm, dout_hbm, wqkv_hbm, wout_hbm, back_ref, resq_ref, reso_ref,
    xv, wqkv, wout, up, std, proj, gat, probs, branch, hold, nt, nall, at, pa, ut, pu, gp, gall,
    ob, rob, tb, ub, sum_o, zs_o, zr_o, kept_o, hs_o, hr_o,
    s2, r2, sum_q, zs_q, zr_q, kept_q, hs_q, hr_q,
    load, sp_s, sp_r, pair_s, pair_r, bk_s, bk_r, n_s, n_r, gx_s, gx_r, fw_s, fw_r,
    ob_s, ob_r, y_s, y_r, x2_s, x2_r, z_s, z_r,
):
    dp, seq = lax.axis_index("dp"), lax.axis_index("seq")
    y, zl, core, x, zh = dp // 4, (dp // 2) % 2, dp % 2, seq // 4, seq % 4

    def seq_peer(o):
        return {"seq": lax.rem(seq + o, 16)}

    def x_peer(o):
        return {"seq": lax.rem(x + o, 4) * 4 + zh}

    def zh_peer(o):
        return {"seq": x * 4 + lax.rem(zh + o, 4)}

    def y_peer(o):
        return {"dp": lax.rem(y + o, 4) * 4 + zl * 2 + core}

    core_peer = {"dp": dp + 1 - 2 * core}
    zl_peer = {"dp": dp + 2 - 4 * zl}

    def send(src, dst, s_sem, r_sem, peer):
        copy = pltpu.make_async_remote_copy(src_ref=src, dst_ref=dst, send_sem=s_sem, recv_sem=r_sem, device_id=peer)
        copy.start()
        return copy

    def wait(copies):
        for copy in copies:
            copy.wait()

    barrier = pltpu.get_barrier_semaphore()
    for peer in [seq_peer(o) for o in range(1, 16)] + [y_peer(o) for o in range(1, 4)] + [core_peer, zl_peer]:
        pl.semaphore_signal(barrier, inc=1, device_id=peer)
    loads = [
        pltpu.make_async_copy(x_hbm, xv, load.at[0]),
        pltpu.make_async_copy(wqkv_hbm, wqkv, load.at[1]),
        pltpu.make_async_copy(wout_hbm, wout, load.at[2]),
        pltpu.make_async_copy(dout_hbm.at[seq], up.at[seq], load.at[3]),
    ]
    for copy in loads:
        copy.start()
    pl.semaphore_wait(barrier, 20)
    order = (8, 7, 9, 6, 10, 5, 11, 4, 12, 3, 13, 2, 14, 1, 15)
    spread = [
        send(dout_hbm.at[lax.rem(seq + o, 16)], up.at[seq], sp_s.at[o], sp_r.at[o], seq_peer(o)) for o in order
    ]

    loads[0].wait()
    rows = to_rows(xv[...].astype(F32))
    centred = rows - jnp.mean(rows, axis=-1, keepdims=True)
    inverse = lax.rsqrt(jnp.mean(centred * centred, axis=-1, keepdims=True) + EPS)
    standard = centred * inverse
    std[...] = standard
    normed = standard.astype(BF16)
    standard_t = standard.T
    for c in range(2):
        nt[c] = jnp.concatenate(
            [standard_t[HD * (2 * b + c) : HD * (2 * b + c + 1)] for b in range(8)], axis=0
        ).astype(BF16)
    pair_n = send(nt.at[1 - core], nall.at[:, TOK : 2 * TOK], pair_s.at[0], pair_r.at[0], core_peer)
    nall[:, 0:TOK] = nt[core]
    right, left = x_peer(1), x_peer(3)
    loads[1].wait()
    for t in range(3):
        proj[D * t : D * t + D, :] = dot(normed, wqkv[:, D * t : D * t + D]).T
    pair_n.wait()
    both = nall.at[:, 0 : 2 * TOK]
    rows_r = send(both, nall.at[:, 2 * TOK : 4 * TOK], n_s.at[0], n_r.at[0], right)
    rows_l = send(both, nall.at[:, 6 * TOK : 8 * TOK], n_s.at[1], n_r.at[1], left)

    mask = (
        lax.broadcasted_iota(jnp.int32, (8, 128), 0) == lax.broadcasted_iota(jnp.int32, (8, 128), 1) % 8
    ).astype(F32)

    def forward_group(i, carry):
        base = pl.multiple_of(i * 288, 288)
        blocks = [proj[pl.ds(pl.multiple_of(D * t + base, 288), 288), :] for t in range(3)]
        heads = []
        for h in range(4):

            def keep(p, value, h=h):
                probs[i * 4 + h, p] = value

            heads.append(forward_head(*(b[HD * h : HD * h + HD] for b in blocks), mask, keep))
        half = pl.multiple_of(i * 144, 144)
        for c in range(2):
            at[c, pl.ds(half, 144), :] = jnp.concatenate([heads[c], heads[c + 2]], axis=0).astype(BF16)
        return carry

    lax.fori_loop(0, 4, forward_group, 0)
    pair_a = send(at.at[1 - core], pa, pair_s.at[1], pair_r.at[1], core_peer)

    loads[2].wait()
    loads[3].wait()
    wait(spread)
    up_t = to_rows(up[...].astype(F32)).T.astype(BF16)
    ut[...] = up_t
    pair_u = send(ut, pu, pair_s.at[2], pair_r.at[2], core_peer)
    gat[...] = dot(wout[...], up_t)
    wait([pair_a, pair_u])

    own_a = at[core]
    for n in range(3):
        cols = slice(OW * n, OW * n + OW)
        val = (dot(own_a, ut[cols, :], NT) + dot(pa[...], pu[cols, :], NT)).astype(BF16)
        for r in range(4):
            ob[r, :, cols] = val[144 * r : 144 * r + 144]
    out_y = [
        send(ob.at[lax.rem(y + o, 4)], rob.at[o - 1], ob_s.at[o - 1], ob_r.at[o - 1], y_peer(o)) for o in (2, 1, 3)
    ]
    wait([rows_r, rows_l])
    rows_on = [
        send(nall.at[:, 2 * TOK : 3 * TOK], nall.at[:, 4 * TOK : 5 * TOK], n_s.at[2], n_r.at[2], right),
        send(nall.at[:, 7 * TOK : 8 * TOK], nall.at[:, 5 * TOK : 6 * TOK], n_s.at[3], n_r.at[3], left),
    ]


    def columns(g, o, part):
        place = gall.at[pl.ds(pl.multiple_of(part * 288, 32), 288), pl.ds(pl.multiple_of(o * 2 * TOK, 2 * TOK), TOK)]
        return pltpu.make_async_remote_copy(
            src_ref=gp.at[pl.ds(pl.multiple_of(g * 288, 32), 288)],
            dst_ref=place,
            send_sem=gx_s.at[g],
            recv_sem=gx_r.at[(o - 1) * 3 + part],
            device_id=x_peer(o),
        )

    def backward_group(i, carry):
        base = pl.multiple_of(i * 288, 288)
        blocks = [proj[pl.ds(pl.multiple_of(D * t + base, 288), 288), :] for t in range(3)]
        blocks.append(gat[pl.ds(base, 288), :])
        heads = [
            backward_head(*(b[HD * h : HD * h + HD] for b in blocks), lambda p, h=h: probs[i * 4 + h, p])
            for h in range(4)
        ]
        for t in range(3):
            gp[pl.ds(pl.multiple_of(D * t + base, 288), 288), :] = jnp.concatenate(
                [h[t] for h in heads], axis=0
            ).astype(BF16)
            g = 4 * t + i
            o = lax.rem(g // 3 - x + 4, 4)

            @pl.when(o != 0)
            def _():
                columns(g, o, lax.rem(g, 3)).start()

        return carry

    lax.fori_loop(0, 4, backward_group, 0)
    mine = gp.at[pl.ds(pl.multiple_of(x * 864, 32), 864)]
    own_g = pltpu.make_async_copy(mine, gall.at[0:864, 0:TOK], load.at[4])
    own_g.start()
    pair_g = send(mine, gall.at[0:864, TOK : 2 * TOK], fw_s.at[9], fw_r.at[9], core_peer)

    gn = dot(wqkv[...], gp[...]).T
    standard = std[...]
    value = inverse * (
        gn
        - jnp.mean(gn, axis=-1, keepdims=True)
        - standard * jnp.mean(gn * standard, axis=-1, keepdims=True)
    )
    branch[...] = from_rows(value).astype(BF16).reshape(4, 4, PX, D)
    back_z = [
        send(branch.at[:, lax.rem(zh + o, 4)], hold.at[zh], bk_s.at[o - 1], bk_r.at[o - 1], zh_peer(o))
        for o in (2, 1, 3)
    ]
    hold[zh] = branch[:, zh]

    wait(out_y)
    val = add(ob[y], rob[0], rob[1], rob[2]).astype(BF16)
    for b in range(4):
        tb[b, :, 0:288] = val[:, 288 * b : 288 * b + 288]
        tb[b, :, 288:OW] = jnp.zeros((144, OW - 288), BF16)

    wait(rows_on + [pair_g])
    own_g.wait()
    sums_y = []
    for turn in range(3):
        part = lax.rem(turn + x, 3)
        rows = pl.ds(pl.multiple_of(part * 288, 32), 288)
        forwards = []
        for o in (1, 3, 2):
            columns(0, o, part).wait_recv()
            sem = (o - 1) * 3 + part
            forwards.append(
                send(
                    gall.at[rows, 2 * o * TOK : (2 * o + 1) * TOK],
                    gall.at[rows, (2 * o + 1) * TOK : (2 * o + 2) * TOK],
                    fw_s.at[sem], fw_r.at[sem], core_peer,
                )
            )
        if turn == 2:
            later = [
                send(tb.at[lax.rem(x + o, 4)], ub.at[o - 1], x2_s.at[o - 1], x2_r.at[o - 1], x_peer(o))
                for o in (2, 1, 3)
            ]
            wait(back_z)
            back_x = [
                send(
                    hold.at[:, lax.rem(x + o, 4)], back_ref.at[pl.ds(x * 4, 4)],
                    bk_s.at[o + 2], bk_r.at[o + 2], x_peer(o),
                )
                for o in (2, 1, 3)
            ]
            back_ref[pl.ds(x * 4, 4)] = hold[:, x]
        wait(forwards)
        val = dot(nall[...], gall[rows, :], NT)
        val = jnp.concatenate([val, jnp.zeros((HALF, OW - 288), F32)], axis=1).astype(BF16)
        for b in range(4):
            s2[b, part] = val[144 * b : 144 * b + 144]
        for o in (2, 1, 3):
            sem = 3 * turn + o - 1
            sums_y.append(
                send(s2.at[lax.rem(y + o, 4), part], r2.at[o - 1, part], y_s.at[sem], y_r.at[sem], y_peer(o))
            )
    for o in range(1, 4):
        for part in range(3):
            columns(3 * lax.rem(x + o, 4) + part, o, part).wait_send()

    def pair_z(sums, zs, zr, sem):
        zs[...] = sums[pl.ds(pl.multiple_of(64 * (1 - zl), 64), 80), :].astype(BF16)
        return send(zs, zr, z_s.at[sem], z_r.at[sem], zl_peer)

    def four_z(pair, sums, zr, kept, hs, hr, width, sem):
        pair.wait()
        kept[...] = sums[pl.ds(pl.multiple_of(64 * zl, 64), 80), :] + zr[...].astype(F32)
        value = kept[pl.ds(pl.multiple_of(8 * zl, 8), 72), :]
        hs[...] = jnp.zeros_like(hs)
        for b in range(4):
            hs[b, 0:72, 0:width] = value[:, width * b : width * b + width].astype(BF16)
        return [
            send(hs.at[lax.rem(zh + o, 4)], hr.at[o - 1], z_s.at[sem + o], z_r.at[sem + o], zh_peer(o))
            for o in (2, 1, 3)
        ]

    wait(later)
    sum_o[...] = add(tb[x], ub[0], ub[1], ub[2])
    pair_o = pair_z(sum_o, zs_o, zr_o, 0)
    wait(sums_y)
    val = add(s2[y], r2[0], r2[1], r2[2])
    sum_q[...] = jnp.concatenate([val[0, :, 0:288], val[1, :, 0:288], val[2, :, 0:288], jnp.zeros((144, 32), F32)], axis=1)
    pair_q = pair_z(sum_q, zs_q, zr_q, 4)
    four_o = four_z(pair_o, sum_o, zr_o, kept_o, hs_o, hr_o, 72, 0)
    four_q = four_z(pair_q, sum_q, zr_q, kept_q, hs_q, hr_q, 216, 4)
    wait(four_o)
    reso_ref[...] = add(hs_o[zh], hr_o[0], hr_o[1], hr_o[2])
    wait(back_x)
    wait(four_q)
    resq_ref[...] = add(hs_q[zh], hr_q[0], hr_q[1], hr_q[2])


def fused(x, dout, wqkv, wout):
    dma = pltpu.SemaphoreType.DMA

    def buf(*shape, dtype=BF16):
        return pltpu.VMEM(shape, dtype)

    return pl.pallas_call(
        kernel,
        out_shape=[
            jax.ShapeDtypeStruct((16, PX, D), BF16),
            jax.ShapeDtypeStruct((80, 256), F32),
            jax.ShapeDtypeStruct((80, 128), F32),
        ],
        in_specs=[pl.BlockSpec(memory_space=pl.ANY)] * 4,
        out_specs=[pl.BlockSpec(memory_space=pltpu.VMEM)] * 3,
        scratch_shapes=[
            buf(FR, PX, D), buf(D, 3 * D), buf(D, D), buf(16, PX, D),
            buf(TOK, D, dtype=F32), buf(3 * D, TOK, dtype=F32), buf(D, TOK, dtype=F32),
            buf(16, 2, 128, 128, dtype=F32), buf(4, 4, PX, D), buf(4, 4, PX, D),
            buf(2, HALF, TOK), buf(HALF, 8 * TOK), buf(2, HALF, TOK), buf(HALF, TOK),
            buf(D, TOK), buf(D, TOK), buf(3 * D, TOK), buf(864, 8 * TOK),
            buf(4, 144, D), buf(3, 144, D), buf(4, 144, OW), buf(3, 144, OW),
            buf(144, OW, dtype=F32), buf(80, OW), buf(80, OW), buf(80, OW, dtype=F32),
            buf(4, 80, 128), buf(3, 80, 128),
            buf(4, 3, 144, OW), buf(3, 3, 144, OW),
            buf(144, QW, dtype=F32), buf(80, QW), buf(80, QW), buf(80, QW, dtype=F32),
            buf(4, 80, 256), buf(3, 80, 256),
            dma((5,)), dma((16,)), dma((16,)), dma((3,)), dma((3,)), dma((6,)), dma((6,)),
            dma((4,)), dma((4,)), dma((12,)), dma((9,)), dma((10,)), dma((10,)),
            dma((3,)), dma((3,)), dma((9,)), dma((9,)), dma((3,)), dma((3,)), dma((8,)), dma((8,)),
        ],
        compiler_params=pltpu.CompilerParams(
            collective_id=1, has_side_effects=True, vmem_limit_bytes=56 * MIB
        ),
    )(x, dout, wqkv, wout)


def finish_kernel(dout, back, resq, reso, d_x1, g_qkv, g_out):
    d_x1[...] = (dout[...].astype(F32) + back[...].astype(F32)).astype(BF16)
    g_qkv[...] = resq[0:72, 0:216] * (1.0 / 256.0)
    g_out[...] = reso[0:72, 0:72] * (1.0 / 256.0)


def finish(dout, back, resq, reso):
    vmem = pl.BlockSpec(memory_space=pltpu.VMEM)
    return pl.pallas_call(
        finish_kernel,
        out_shape=[
            jax.ShapeDtypeStruct((16, PX, D), BF16),
            jax.ShapeDtypeStruct((72, 216), F32),
            jax.ShapeDtypeStruct((72, 72), F32),
        ],
        in_specs=[vmem] * 4,
        out_specs=[vmem] * 3,
    )(dout, back, resq, reso)


def local(x1_pixels, dout_frames, w_qkv, w_out):
    x = x1_pixels.reshape(FR, PX, D)
    dout = dout_frames.reshape(16, PX, D)
    back, resq, reso = fused(x, dout, w_qkv, w_out)
    d_x1, g_qkv, g_out = finish(dout, back, resq, reso)
    return d_x1.reshape(dout_frames.shape), g_qkv, g_out


def solution(mesh):
    return jax.shard_map(
        local,
        mesh=mesh,
        in_specs=(P("dp", None, "seq", None), P("dp", "seq", None, None), P(), P()),
        out_specs=(P("dp", "seq", None, None), P("dp", "seq"), P("dp", "seq")),
        check_vma=False,
    )
```

```python
import jax
import jax.numpy as jnp
from jax import lax
from jax.experimental import pallas as pl
from jax.experimental.pallas import tpu as pltpu
from jax.sharding import PartitionSpec as P

F32, BF16 = jnp.float32, jnp.bfloat16
EPS = 1e-06
HD = 72
D = 1152
HALF = D // 2
FR = 16
PX = 16
TOK = FR * PX
FACTOR = HD**-0.5
NT = (((1,), (1,)), ((), ()))
TN = (((0,), (0,)), ((), ()))
QW, OW = 896, 384
MIB = 1 << 20


def dot(a, b, dims=None):
    if dims is None:
        return jnp.dot(a, b, preferred_element_type=F32)
    return lax.dot_general(a, b, dims, preferred_element_type=F32)


def to_rows(block):
    return jnp.concatenate([block[:, 8 * p : 8 * p + 8, :].reshape(128, D) for p in range(2)], axis=0)


def from_rows(rows):
    return jnp.concatenate([rows[128 * p : 128 * p + 128].reshape(FR, 8, D) for p in range(2)], axis=1)


def head_scale(v):
    return lax.rsqrt(jnp.sum(v * v, axis=0, keepdims=True) * (1.0 / HD) + EPS)


def forward_head(q, k, v, mask, keep):
    qn, kn, vb = (q * head_scale(q)).astype(BF16), (k * head_scale(k)).astype(BF16), v.astype(BF16)
    out = []
    for p in range(2):
        at = slice(128 * p, 128 * p + 128)
        e = jnp.exp(dot(kn[:, at], qn[:, at], TN) * FACTOR).reshape(FR, 8, 128)
        probs = (e * (mask / jnp.sum(e, axis=0))[None]).reshape(128, 128)
        keep(p, probs)
        out.append(dot(vb[:, at], probs.astype(BF16)))
    return jnp.concatenate(out, axis=1)


def backward_head(q, k, v, ga, probs_of):
    rq, rk = head_scale(q), head_scale(k)
    qn, kn = (q * rq).astype(BF16), (k * rk).astype(BF16)
    vb, gb = v.astype(BF16), ga.astype(BF16)
    out = []
    for p in range(2):
        at = slice(128 * p, 128 * p + 128)
        qh, kh, vh, gh = qn[:, at], kn[:, at], vb[:, at], gb[:, at]
        flat = probs_of(p)
        probs = flat.reshape(FR, 8, 128)
        pb = flat.astype(BF16)
        grad_probs = dot(vh, gh, TN).reshape(FR, 8, 128)
        total = jnp.sum(probs * grad_probs, axis=0)
        gs = (probs * (grad_probs - total[None]) * FACTOR).reshape(128, 128).astype(BF16)
        out.append((dot(kh, gs), dot(qh, gs, NT), dot(gh, pb, NT)))
    gqn, gkn, gv = (jnp.concatenate(pair, axis=1) for pair in zip(*out))
    tq = jnp.sum(gqn * q, axis=0, keepdims=True) * (1.0 / HD)
    tk = jnp.sum(gkn * k, axis=0, keepdims=True) * (1.0 / HD)
    gq = rq * gqn - q * (rq * rq * rq * tq)
    gk = rk * gkn - k * (rk * rk * rk * tk)
    return gq, gk, gv


def add(own, *others):
    value = own.astype(F32)
    for other in others:
        value = value + other.astype(F32)
    return value


def kernel(
    x_hbm, dout_hbm, wqkv_hbm, wout_hbm, d_x1_ref, resq_ref, reso_ref,
    xv, wqkv, wout, up, std, proj, gat, probs, branch, hold, back, nt, nall, at, pa, ut, pu, gp, gall,
    ob, rob, tb, ub, sum_o, zs_o, zr_o, kept_o, hs_o, hr_o,
    s2, r2, sum_q, zs_q, zr_q, kept_q, hs_q, hr_q,
    load, sp_s, sp_r, pair_s, pair_r, bk_s, bk_r, n_s, n_r, gx_s, gx_r, fw_s, fw_r,
    ob_s, ob_r, y_s, y_r, x2_s, x2_r, z_s, z_r,
):
    dp, seq = lax.axis_index("dp"), lax.axis_index("seq")
    y, zl, core, x, zh = dp // 4, (dp // 2) % 2, dp % 2, seq // 4, seq % 4

    def seq_peer(o):
        return {"seq": lax.rem(seq + o, 16)}

    def x_peer(o):
        return {"seq": lax.rem(x + o, 4) * 4 + zh}

    def zh_peer(o):
        return {"seq": x * 4 + lax.rem(zh + o, 4)}

    def y_peer(o):
        return {"dp": lax.rem(y + o, 4) * 4 + zl * 2 + core}

    core_peer = {"dp": dp + 1 - 2 * core}
    zl_peer = {"dp": dp + 2 - 4 * zl}

    def send(src, dst, s_sem, r_sem, peer):
        copy = pltpu.make_async_remote_copy(src_ref=src, dst_ref=dst, send_sem=s_sem, recv_sem=r_sem, device_id=peer)
        copy.start()
        return copy

    def wait(copies):
        for copy in copies:
            copy.wait()

    barrier = pltpu.get_barrier_semaphore()
    for peer in [seq_peer(o) for o in range(1, 16)] + [y_peer(o) for o in range(1, 4)] + [core_peer, zl_peer]:
        pl.semaphore_signal(barrier, inc=1, device_id=peer)
    loads = [
        pltpu.make_async_copy(x_hbm, xv, load.at[0]),
        pltpu.make_async_copy(wqkv_hbm, wqkv, load.at[1]),
        pltpu.make_async_copy(wout_hbm, wout, load.at[2]),
        pltpu.make_async_copy(dout_hbm.at[seq], up.at[seq], load.at[3]),
    ]
    for copy in loads:
        copy.start()
    pl.semaphore_wait(barrier, 20)
    order = (8, 7, 9, 6, 10, 5, 11, 4, 12, 3, 13, 2, 14, 1, 15)
    spread = [
        send(dout_hbm.at[lax.rem(seq + o, 16)], up.at[seq], sp_s.at[o], sp_r.at[o], seq_peer(o)) for o in order
    ]

    loads[0].wait()
    rows = to_rows(xv[...].astype(F32))
    centred = rows - jnp.mean(rows, axis=-1, keepdims=True)
    inverse = lax.rsqrt(jnp.mean(centred * centred, axis=-1, keepdims=True) + EPS)
    standard = centred * inverse
    std[...] = standard
    normed = standard.astype(BF16)
    standard_t = standard.T
    for c in range(2):
        nt[c] = jnp.concatenate(
            [standard_t[HD * (2 * b + c) : HD * (2 * b + c + 1)] for b in range(8)], axis=0
        ).astype(BF16)
    pair_n = send(nt.at[1 - core], nall.at[:, TOK : 2 * TOK], pair_s.at[0], pair_r.at[0], core_peer)
    nall[:, 0:TOK] = nt[core]
    right, left = x_peer(1), x_peer(3)
    pair_n.wait()
    both = nall.at[:, 0 : 2 * TOK]
    rows_r = send(both, nall.at[:, 2 * TOK : 4 * TOK], n_s.at[0], n_r.at[0], right)
    rows_l = send(both, nall.at[:, 6 * TOK : 8 * TOK], n_s.at[1], n_r.at[1], left)
    loads[1].wait()
    for t in range(3):
        proj[D * t : D * t + D, :] = dot(normed, wqkv[:, D * t : D * t + D]).T

    mask = (
        lax.broadcasted_iota(jnp.int32, (8, 128), 0) == lax.broadcasted_iota(jnp.int32, (8, 128), 1) % 8
    ).astype(F32)

    def forward_group(i, carry):
        base = pl.multiple_of(i * 288, 288)
        blocks = [proj[pl.ds(pl.multiple_of(D * t + base, 288), 288), :] for t in range(3)]
        heads = []
        for h in range(4):

            def keep(p, value, h=h):
                probs[i * 4 + h, p] = value

            heads.append(forward_head(*(b[HD * h : HD * h + HD] for b in blocks), mask, keep))
        half = pl.multiple_of(i * 144, 144)
        for c in range(2):
            at[c, pl.ds(half, 144), :] = jnp.concatenate([heads[c], heads[c + 2]], axis=0).astype(BF16)
        return carry

    lax.fori_loop(0, 4, forward_group, 0)
    pair_a = send(at.at[1 - core], pa, pair_s.at[1], pair_r.at[1], core_peer)

    hs_o[...] = jnp.zeros_like(hs_o)
    hs_q[...] = jnp.zeros_like(hs_q)

    loads[2].wait()
    loads[3].wait()
    wait(spread)
    up_t = to_rows(up[...].astype(F32)).T.astype(BF16)
    ut[...] = up_t
    pair_u = send(ut, pu, pair_s.at[2], pair_r.at[2], core_peer)
    gat[...] = dot(wout[...], up_t)
    wait([pair_a, pair_u])

    own_a = at[core]
    for n in range(3):
        cols = slice(OW * n, OW * n + OW)
        val = (dot(own_a, ut[cols, :], NT) + dot(pa[...], pu[cols, :], NT)).astype(BF16)
        for r in range(4):
            ob[r, :, cols] = val[144 * r : 144 * r + 144]
    out_y = [
        send(ob.at[lax.rem(y + o, 4)], rob.at[o - 1], ob_s.at[o - 1], ob_r.at[o - 1], y_peer(o)) for o in (2, 1, 3)
    ]
    wait([rows_r, rows_l])
    rows_on = [
        send(nall.at[:, 2 * TOK : 3 * TOK], nall.at[:, 4 * TOK : 5 * TOK], n_s.at[2], n_r.at[2], right),
        send(nall.at[:, 7 * TOK : 8 * TOK], nall.at[:, 5 * TOK : 6 * TOK], n_s.at[3], n_r.at[3], left),
    ]


    def columns(o, turn):
        xd = lax.rem(x + o, 4)
        part = lax.rem(turn + xd, 3)
        return pltpu.make_async_remote_copy(
            src_ref=gp.at[pl.ds(pl.multiple_of((3 * xd + part) * 288, 32), 288)],
            dst_ref=gall.at[pl.ds(pl.multiple_of(part * 288, 32), 288), 2 * o * TOK : (2 * o + 1) * TOK],
            send_sem=gx_s.at[3 * (o - 1) + turn],
            recv_sem=gx_r.at[3 * (o - 1) + turn],
            device_id=x_peer(o),
        )

    def issue(turn):
        for o in (2, 1, 3):
            columns(o, turn).start()

    def backward_group(i, carry):
        base = pl.multiple_of(i * 288, 288)
        blocks = [proj[pl.ds(pl.multiple_of(D * t + base, 288), 288), :] for t in range(3)]
        blocks.append(gat[pl.ds(base, 288), :])
        heads = [
            backward_head(*(b[HD * h : HD * h + HD] for b in blocks), lambda p, h=h: probs[i * 4 + h, p])
            for h in range(4)
        ]
        for t in range(3):
            gp[pl.ds(pl.multiple_of(D * t + base, 288), 288), :] = jnp.concatenate(
                [h[t] for h in heads], axis=0
            ).astype(BF16)
        return carry

    lax.fori_loop(0, 2, backward_group, 0)
    issue(0)
    lax.fori_loop(2, 4, backward_group, 0)
    issue(1)
    mine = gp.at[pl.ds(pl.multiple_of(x * 864, 32), 864)]
    own_g = pltpu.make_async_copy(mine, gall.at[0:864, 0:TOK], load.at[4])
    own_g.start()
    pair_g = send(mine, gall.at[0:864, TOK : 2 * TOK], fw_s.at[9], fw_r.at[9], core_peer)

    gn = dot(wqkv[...], gp[...]).T
    standard = std[...]
    value = inverse * (
        gn
        - jnp.mean(gn, axis=-1, keepdims=True)
        - standard * jnp.mean(gn * standard, axis=-1, keepdims=True)
    )
    branch[...] = from_rows(value).astype(BF16).reshape(4, 4, PX, D)
    back_z = [
        send(branch.at[:, lax.rem(zh + o, 4)], hold.at[zh], bk_s.at[o - 1], bk_r.at[o - 1], zh_peer(o))
        for o in (2, 1, 3)
    ]
    hold[zh] = branch[:, zh]

    for o in (2, 1, 3):
        columns(o, 0).wait_send()
    issue(2)

    wait(out_y)
    val = add(ob[y], rob[0], rob[1], rob[2]).astype(BF16)
    for b in range(4):
        tb[b, :, 0:288] = val[:, 288 * b : 288 * b + 288]
        tb[b, :, 288:OW] = jnp.zeros((144, OW - 288), BF16)

    own_d = pltpu.make_async_copy(dout_hbm, up, load.at[3])
    own_d.start()

    wait(rows_on + [pair_g])
    own_g.wait()
    sums_y = []

    def pair_z(turn):
        wait(sums_y[turn])
        part = lax.rem(turn + x, 3)
        sum_q[part] = add(s2[y, part], r2[0, part], r2[1, part], r2[2, part])
        zs_q[part] = sum_q[part, pl.ds(pl.multiple_of(64 * (1 - zl), 64), 80), :].astype(BF16)
        return send(zs_q.at[part], zr_q.at[part], z_s.at[turn + 4], z_r.at[turn + 4], zl_peer)

    pairs_q = []
    for turn in range(3):
        part = lax.rem(turn + x, 3)
        rows = pl.ds(pl.multiple_of(part * 288, 32), 288)
        forwards = []
        for o in (1, 3, 2):
            columns(o, turn).wait_recv()
            sem = (o - 1) * 3 + turn
            forwards.append(
                send(
                    gall.at[rows, 2 * o * TOK : (2 * o + 1) * TOK],
                    gall.at[rows, (2 * o + 1) * TOK : (2 * o + 2) * TOK],
                    fw_s.at[sem], fw_r.at[sem], core_peer,
                )
            )
        wait(forwards)
        val = dot(nall[...], gall[rows, :], NT)
        val = jnp.concatenate([val, jnp.zeros((HALF, OW - 288), F32)], axis=1).astype(BF16)
        for b in range(4):
            s2[b, part] = val[144 * b : 144 * b + 144]
        sums_y.append(
            [
                send(
                    s2.at[lax.rem(y + o, 4), part], r2.at[o - 1, part],
                    y_s.at[3 * turn + o - 1], y_r.at[3 * turn + o - 1], y_peer(o),
                )
                for o in (2, 1, 3)
            ]
        )
        if turn == 1:
            pairs_q.append(pair_z(0))
    for o in (2, 1, 3):
        columns(o, 1).wait_send()
        columns(o, 2).wait_send()
    later = [
        send(tb.at[lax.rem(x + o, 4)], ub.at[o - 1], x2_s.at[o - 1], x2_r.at[o - 1], x_peer(o)) for o in (2, 1, 3)
    ]
    wait(back_z)
    back_x = [
        send(
            hold.at[:, lax.rem(x + o, 4)], back.at[pl.ds(x * 4, 4)], bk_s.at[o + 2], bk_r.at[o + 2], x_peer(o)
        )
        for o in (2, 1, 3)
    ]
    back[pl.ds(x * 4, 4)] = hold[:, x]
    pairs_q.append(pair_z(1))

    wait(later)
    sum_o[...] = add(tb[x], ub[0], ub[1], ub[2])
    zs_o[...] = sum_o[pl.ds(pl.multiple_of(64 * (1 - zl), 64), 80), :].astype(BF16)
    pair_o = send(zs_o, zr_o, z_s.at[0], z_r.at[0], zl_peer)
    pairs_q.append(pair_z(2))

    def four_z(value, hs, hr, width, sem):
        for b in range(4):
            hs[b, 0:72, 0:width] = value[:, width * b : width * b + width].astype(BF16)
        return [
            send(hs.at[lax.rem(zh + o, 4)], hr.at[o - 1], z_s.at[sem + o], z_r.at[sem + o], zh_peer(o))
            for o in (2, 1, 3)
        ]

    window = pl.ds(pl.multiple_of(64 * zl, 64), 80)
    inner = pl.ds(pl.multiple_of(8 * zl, 8), 72)
    pair_o.wait()
    kept_o[...] = sum_o[window, :] + zr_o[...].astype(F32)
    four_o = four_z(kept_o[inner, :], hs_o, hr_o, 72, 0)
    wait(pairs_q)
    for part in range(3):
        kept_q[part] = sum_q[part, window, :] + zr_q[part].astype(F32)
    four_q = four_z(jnp.concatenate([kept_q[part, inner, 0:288] for part in range(3)], axis=1), hs_q, hr_q, 216, 6)
    wait(back_x)
    own_d.wait()
    d_x1_ref[...] = (up[...].astype(F32) + back[...].astype(F32)).astype(BF16)
    wait(four_o)
    reso_ref[...] = add(hs_o[zh], hr_o[0], hr_o[1], hr_o[2])
    wait(four_q)
    resq_ref[...] = add(hs_q[zh], hr_q[0], hr_q[1], hr_q[2])


def fused(x, dout, wqkv, wout):
    dma = pltpu.SemaphoreType.DMA

    def buf(*shape, dtype=BF16):
        return pltpu.VMEM(shape, dtype)

    return pl.pallas_call(
        kernel,
        out_shape=[
            jax.ShapeDtypeStruct((16, PX, D), BF16),
            jax.ShapeDtypeStruct((80, 256), F32),
            jax.ShapeDtypeStruct((80, 128), F32),
        ],
        in_specs=[pl.BlockSpec(memory_space=pl.ANY)] * 4,
        out_specs=[pl.BlockSpec(memory_space=pltpu.VMEM)] * 3,
        scratch_shapes=[
            buf(FR, PX, D), buf(D, 3 * D), buf(D, D), buf(16, PX, D),
            buf(TOK, D, dtype=F32), buf(3 * D, TOK, dtype=F32), buf(D, TOK, dtype=F32),
            buf(16, 2, 128, 128, dtype=F32), buf(4, 4, PX, D), buf(4, 4, PX, D), buf(16, PX, D),
            buf(2, HALF, TOK), buf(HALF, 8 * TOK), buf(2, HALF, TOK), buf(HALF, TOK),
            buf(D, TOK), buf(D, TOK), buf(3 * D, TOK), buf(864, 8 * TOK),
            buf(4, 144, D), buf(3, 144, D), buf(4, 144, OW), buf(3, 144, OW),
            buf(144, OW, dtype=F32), buf(80, OW), buf(80, OW), buf(80, OW, dtype=F32),
            buf(4, 80, 128), buf(3, 80, 128),
            buf(4, 3, 144, OW), buf(3, 3, 144, OW),
            buf(3, 144, OW, dtype=F32), buf(3, 80, OW), buf(3, 80, OW), buf(3, 80, OW, dtype=F32),
            buf(4, 80, 256), buf(3, 80, 256),
            dma((5,)), dma((16,)), dma((16,)), dma((3,)), dma((3,)), dma((6,)), dma((6,)),
            dma((4,)), dma((4,)), dma((9,)), dma((9,)), dma((10,)), dma((10,)),
            dma((3,)), dma((3,)), dma((9,)), dma((9,)), dma((3,)), dma((3,)), dma((10,)), dma((10,)),
        ],
        compiler_params=pltpu.CompilerParams(
            collective_id=1, has_side_effects=True, vmem_limit_bytes=56 * MIB
        ),
    )(x, dout, wqkv, wout)


def finish_kernel(d_x1, resq, reso, out, g_qkv, g_out):
    out[...] = d_x1[...]
    g_qkv[...] = resq[0:72, 0:216] * (1.0 / 256.0)
    g_out[...] = reso[0:72, 0:72] * (1.0 / 256.0)


def finish(d_x1, resq, reso):
    vmem = pl.BlockSpec(memory_space=pltpu.VMEM)
    return pl.pallas_call(
        finish_kernel,
        out_shape=[
            jax.ShapeDtypeStruct((16, PX, D), BF16),
            jax.ShapeDtypeStruct((72, 216), F32),
            jax.ShapeDtypeStruct((72, 72), F32),
        ],
        in_specs=[vmem] * 3,
        out_specs=[vmem] * 3,
    )(d_x1, resq, reso)


def local(x1_pixels, dout_frames, w_qkv, w_out):
    x = x1_pixels.reshape(FR, PX, D)
    dout = dout_frames.reshape(16, PX, D)
    d_x1, g_qkv, g_out = finish(*fused(x, dout, w_qkv, w_out))
    return d_x1.reshape(dout_frames.shape), g_qkv, g_out


def solution(mesh):
    return jax.shard_map(
        local,
        mesh=mesh,
        in_specs=(P("dp", None, "seq", None), P("dp", "seq", None, None), P(), P()),
        out_specs=(P("dp", "seq", None, None), P("dp", "seq"), P("dp", "seq")),
        check_vma=False,
    )
```

```python
import jax
import jax.numpy as jnp
from jax import lax
from jax.experimental import pallas as pl
from jax.experimental.pallas import tpu as pltpu
from jax.sharding import PartitionSpec as P

F32, BF16 = jnp.float32, jnp.bfloat16
EPS = 1e-06
HD = 72
D = 1152
HALF = D // 2
FR = 16
PX = 16
TOK = FR * PX
FACTOR = HD**-0.5
NT = (((1,), (1,)), ((), ()))
TN = (((0,), (0,)), ((), ()))
QW, OW = 896, 384
MIB = 1 << 20


def dot(a, b, dims=None):
    if dims is None:
        return jnp.dot(a, b, preferred_element_type=F32)
    return lax.dot_general(a, b, dims, preferred_element_type=F32)


def to_rows(block):
    return jnp.concatenate([block[:, 8 * p : 8 * p + 8, :].reshape(128, D) for p in range(2)], axis=0)


def from_rows(rows):
    return jnp.concatenate([rows[128 * p : 128 * p + 128].reshape(FR, 8, D) for p in range(2)], axis=1)


def head_scale(v):
    return lax.rsqrt(jnp.sum(v * v, axis=0, keepdims=True) * (1.0 / HD) + EPS)


def forward_head(q, k, v, mask, keep):
    qn, kn, vb = (q * head_scale(q)).astype(BF16), (k * head_scale(k)).astype(BF16), v.astype(BF16)
    out = []
    for p in range(2):
        at = slice(128 * p, 128 * p + 128)
        e = jnp.exp(dot(kn[:, at], qn[:, at], TN) * FACTOR).reshape(FR, 8, 128)
        probs = (e * (mask / jnp.sum(e, axis=0))[None]).reshape(128, 128)
        keep(p, probs)
        out.append(dot(vb[:, at], probs.astype(BF16)))
    return jnp.concatenate(out, axis=1)


def backward_head(q, k, v, ga, probs_of):
    rq, rk = head_scale(q), head_scale(k)
    qn, kn = (q * rq).astype(BF16), (k * rk).astype(BF16)
    vb, gb = v.astype(BF16), ga.astype(BF16)
    out = []
    for p in range(2):
        at = slice(128 * p, 128 * p + 128)
        qh, kh, vh, gh = qn[:, at], kn[:, at], vb[:, at], gb[:, at]
        flat = probs_of(p)
        probs = flat.reshape(FR, 8, 128)
        pb = flat.astype(BF16)
        grad_probs = dot(vh, gh, TN).reshape(FR, 8, 128)
        total = jnp.sum(probs * grad_probs, axis=0)
        gs = (probs * (grad_probs - total[None]) * FACTOR).reshape(128, 128).astype(BF16)
        out.append((dot(kh, gs), dot(qh, gs, NT), dot(gh, pb, NT)))
    gqn, gkn, gv = (jnp.concatenate(pair, axis=1) for pair in zip(*out))
    tq = jnp.sum(gqn * q, axis=0, keepdims=True) * (1.0 / HD)
    tk = jnp.sum(gkn * k, axis=0, keepdims=True) * (1.0 / HD)
    gq = rq * gqn - q * (rq * rq * rq * tq)
    gk = rk * gkn - k * (rk * rk * rk * tk)
    return gq, gk, gv


def add(own, *others):
    value = own.astype(F32)
    for other in others:
        value = value + other.astype(F32)
    return value


def kernel(
    x_hbm, dout_hbm, wqkv_hbm, wout_hbm, d_x1_ref, resq_ref, reso_ref,
    xv, wqkv, wout, up, std, proj, gat, probs, branch, hold, back, nt, nall, at, pa, ut, pu, gp, gall,
    ob, rob, tb, ub, sum_o, zs_o, zr_o, kept_o, hs_o, hr_o,
    s2, r2, r3, sum_q, zs_q, zr_q, kept_q, hs_q, hr_q,
    load, sp_s, sp_r, pair_s, pair_r, bk_s, bk_r, n_s, n_r, gx_s, gx_r, fw_s, fw_r,
    ob_s, ob_r, y_s, y_r, d_s, d_r, x2_s, x2_r, z_s, z_r,
):
    dp, seq = lax.axis_index("dp"), lax.axis_index("seq")
    y, zl, core, x, zh = dp // 4, (dp // 2) % 2, dp % 2, seq // 4, seq % 4

    def seq_peer(o):
        return {"seq": lax.rem(seq + o, 16)}

    def x_peer(o):
        return {"seq": lax.rem(x + o, 4) * 4 + zh}

    def zh_peer(o):
        return {"seq": x * 4 + lax.rem(zh + o, 4)}

    def y_peer(o):
        return {"dp": lax.rem(y + o, 4) * 4 + zl * 2 + core}

    core_peer = {"dp": dp + 1 - 2 * core}
    zl_peer = {"dp": dp + 2 - 4 * zl}

    def send(src, dst, s_sem, r_sem, peer):
        copy = pltpu.make_async_remote_copy(src_ref=src, dst_ref=dst, send_sem=s_sem, recv_sem=r_sem, device_id=peer)
        copy.start()
        return copy

    def wait(copies):
        for copy in copies:
            copy.wait()

    barrier = pltpu.get_barrier_semaphore()
    across = [{"dp": lax.rem(y + o, 4) * 4 + 2 * (1 - zl) + core} for o in range(1, 4)]
    for peer in [seq_peer(o) for o in range(1, 16)] + [y_peer(o) for o in range(1, 4)] + across + [core_peer, zl_peer]:
        pl.semaphore_signal(barrier, inc=1, device_id=peer)
    loads = [
        pltpu.make_async_copy(x_hbm, xv, load.at[0]),
        pltpu.make_async_copy(wqkv_hbm, wqkv, load.at[1]),
        pltpu.make_async_copy(wout_hbm, wout, load.at[2]),
        pltpu.make_async_copy(dout_hbm.at[seq], up.at[seq], load.at[3]),
    ]
    for copy in loads:
        copy.start()
    pl.semaphore_wait(barrier, 23)
    order = (8, 7, 9, 6, 10, 5, 11, 4, 12, 3, 13, 2, 14, 1, 15)
    spread = [
        send(dout_hbm.at[lax.rem(seq + o, 16)], up.at[seq], sp_s.at[o], sp_r.at[o], seq_peer(o)) for o in order
    ]

    loads[0].wait()
    rows = to_rows(xv[...].astype(F32))
    centred = rows - jnp.mean(rows, axis=-1, keepdims=True)
    inverse = lax.rsqrt(jnp.mean(centred * centred, axis=-1, keepdims=True) + EPS)
    standard = centred * inverse
    std[...] = standard
    normed = standard.astype(BF16)
    standard_t = standard.T
    for c in range(2):
        nt[c] = jnp.concatenate(
            [standard_t[HD * (2 * b + c) : HD * (2 * b + c + 1)] for b in range(8)], axis=0
        ).astype(BF16)
    pair_n = send(nt.at[1 - core], nall.at[:, TOK : 2 * TOK], pair_s.at[0], pair_r.at[0], core_peer)
    nall[:, 0:TOK] = nt[core]
    right, left = x_peer(1), x_peer(3)
    pair_n.wait()
    own_rows, pair_rows = nall.at[:, 0:TOK], nall.at[:, TOK : 2 * TOK]
    rows_first = [
        send(own_rows, nall.at[:, 2 * TOK : 3 * TOK], n_s.at[0], n_r.at[0], right),
        send(pair_rows, nall.at[:, 7 * TOK : 8 * TOK], n_s.at[1], n_r.at[1], left),
    ]
    loads[1].wait()
    for t in range(3):
        proj[D * t : D * t + D, :] = dot(normed, wqkv[:, D * t : D * t + D]).T

    mask = (
        lax.broadcasted_iota(jnp.int32, (8, 128), 0) == lax.broadcasted_iota(jnp.int32, (8, 128), 1) % 8
    ).astype(F32)

    def forward_group(i, carry):
        base = pl.multiple_of(i * 288, 288)
        blocks = [proj[pl.ds(pl.multiple_of(D * t + base, 288), 288), :] for t in range(3)]
        heads = []
        for h in range(4):

            def keep(p, value, h=h):
                probs[i * 4 + h, p] = value

            heads.append(forward_head(*(b[HD * h : HD * h + HD] for b in blocks), mask, keep))
        half = pl.multiple_of(i * 144, 144)
        for c in range(2):
            at[c, pl.ds(half, 144), :] = jnp.concatenate([heads[c], heads[c + 2]], axis=0).astype(BF16)
        return carry

    lax.fori_loop(0, 4, forward_group, 0)
    pair_a = send(at.at[1 - core], pa, pair_s.at[1], pair_r.at[1], core_peer)

    wait(rows_first)
    rows_on = [
        send(nall.at[:, 2 * TOK : 3 * TOK], nall.at[:, 4 * TOK : 5 * TOK], n_s.at[2], n_r.at[2], right),
        send(nall.at[:, 7 * TOK : 8 * TOK], nall.at[:, 5 * TOK : 6 * TOK], n_s.at[3], n_r.at[3], left),
        send(pair_rows, nall.at[:, 3 * TOK : 4 * TOK], n_s.at[4], n_r.at[4], right),
        send(own_rows, nall.at[:, 6 * TOK : 7 * TOK], n_s.at[5], n_r.at[5], left),
    ]
    hs_o[...] = jnp.zeros_like(hs_o)
    hs_q[...] = jnp.zeros_like(hs_q)

    loads[2].wait()
    loads[3].wait()
    wait(spread)
    up_t = to_rows(up[...].astype(F32)).T.astype(BF16)
    ut[...] = up_t
    pair_u = send(ut, pu, pair_s.at[2], pair_r.at[2], core_peer)
    gat[...] = dot(wout[...], up_t)
    wait([pair_a, pair_u])

    own_a = at[core]
    for n in range(3):
        cols = slice(OW * n, OW * n + OW)
        val = (dot(own_a, ut[cols, :], NT) + dot(pa[...], pu[cols, :], NT)).astype(BF16)
        for r in range(4):
            ob[r, :, cols] = val[144 * r : 144 * r + 144]
    out_y = [
        send(ob.at[lax.rem(y + o, 4)], rob.at[o - 1], ob_s.at[o - 1], ob_r.at[o - 1], y_peer(o)) for o in (2, 1, 3)
    ]


    def columns(o, turn):
        xd = lax.rem(x + o, 4)
        part = lax.rem(turn + xd, 3)
        return pltpu.make_async_remote_copy(
            src_ref=gp.at[pl.ds(pl.multiple_of((3 * xd + part) * 288, 32), 288)],
            dst_ref=gall.at[pl.ds(pl.multiple_of(part * 288, 32), 288), 2 * o * TOK : (2 * o + 1) * TOK],
            send_sem=gx_s.at[3 * (o - 1) + turn],
            recv_sem=gx_r.at[3 * (o - 1) + turn],
            device_id=x_peer(o),
        )

    def issue(turn):
        for o in (2, 1, 3):
            columns(o, turn).start()

    def backward_group(i, carry):
        base = pl.multiple_of(i * 288, 288)
        blocks = [proj[pl.ds(pl.multiple_of(D * t + base, 288), 288), :] for t in range(3)]
        blocks.append(gat[pl.ds(base, 288), :])
        heads = [
            backward_head(*(b[HD * h : HD * h + HD] for b in blocks), lambda p, h=h: probs[i * 4 + h, p])
            for h in range(4)
        ]
        for t in range(3):
            gp[pl.ds(pl.multiple_of(D * t + base, 288), 288), :] = jnp.concatenate(
                [h[t] for h in heads], axis=0
            ).astype(BF16)
        return carry

    lax.fori_loop(0, 2, backward_group, 0)
    issue(0)
    lax.fori_loop(2, 4, backward_group, 0)
    issue(1)
    mine = gp.at[pl.ds(pl.multiple_of(x * 864, 32), 864)]
    own_g = pltpu.make_async_copy(mine, gall.at[0:864, 0:TOK], load.at[4])
    own_g.start()
    pair_g = send(mine, gall.at[0:864, TOK : 2 * TOK], fw_s.at[9], fw_r.at[9], core_peer)

    gn = dot(wqkv[...], gp[...]).T
    standard = std[...]
    value = inverse * (
        gn
        - jnp.mean(gn, axis=-1, keepdims=True)
        - standard * jnp.mean(gn * standard, axis=-1, keepdims=True)
    )
    branch[...] = from_rows(value).astype(BF16).reshape(4, 4, PX, D)
    back_z = [
        send(branch.at[:, lax.rem(zh + o, 4)], hold.at[zh], bk_s.at[o - 1], bk_r.at[o - 1], zh_peer(o))
        for o in (2, 1, 3)
    ]
    hold[zh] = branch[:, zh]

    for o in (2, 1, 3):
        columns(o, 0).wait_send()
    issue(2)

    wait(out_y)
    val = add(ob[y], rob[0], rob[1], rob[2]).astype(BF16)
    for b in range(4):
        tb[b, :, 0:288] = val[:, 288 * b : 288 * b + 288]
        tb[b, :, 288:OW] = jnp.zeros((144, OW - 288), BF16)

    own_d = pltpu.make_async_copy(dout_hbm, up, load.at[3])
    own_d.start()

    wait(rows_on + [pair_g])
    own_g.wait()
    sums_y = []

    def pair_z(turn):
        wait(sums_y[turn])
        part = lax.rem(turn + x, 3)
        sum_q[part] = add(s2[y, part], r2[0, part], r2[1, part], r2[2, part])
        zs_q[part] = sum_q[part, pl.ds(pl.multiple_of(64 * (1 - zl), 64), 80), :].astype(BF16)
        return send(zs_q.at[part], zr_q.at[part], z_s.at[turn + 4], z_r.at[turn + 4], zl_peer)

    pairs_q = []
    for turn in range(3):
        part = lax.rem(turn + x, 3)
        rows = pl.ds(pl.multiple_of(part * 288, 32), 288)
        forwards = []
        for o in (1, 3, 2):
            columns(o, turn).wait_recv()
            sem = (o - 1) * 3 + turn
            forwards.append(
                send(
                    gall.at[rows, 2 * o * TOK : (2 * o + 1) * TOK],
                    gall.at[rows, (2 * o + 1) * TOK : (2 * o + 2) * TOK],
                    fw_s.at[sem], fw_r.at[sem], core_peer,
                )
            )
        wait(forwards)
        val = dot(nall[...], gall[rows, :], NT)
        val = jnp.concatenate([val, jnp.zeros((HALF, OW - 288), F32)], axis=1).astype(BF16)
        for b in range(4):
            s2[b, part] = val[144 * b : 144 * b + 144]
        if turn < 2:
            sums_y.append(
                [
                    send(
                        s2.at[lax.rem(y + o, 4), part], r2.at[o - 1, part],
                        y_s.at[3 * turn + o - 1], y_r.at[3 * turn + o - 1], y_peer(o),
                    )
                    for o in (2, 1, 3)
                ]
            )
        if turn == 1:
            pairs_q.append(pair_z(0))
            later = [
                send(tb.at[lax.rem(x + o, 4)], ub.at[o - 1], x2_s.at[o - 1], x2_r.at[o - 1], x_peer(o)) for o in (2, 1, 3)
            ]
    last = lax.rem(2 + x, 3)
    direct = []
    for o, oz in ((2, 1), (2, 0), (1, 1), (1, 0), (3, 1), (3, 0), (0, 1)):
        yd, zd, sem = lax.rem(y + o, 4), (zl if oz == 0 else 1 - zl), 2 * o + oz - 1
        piece = s2.at[yd, last, pl.ds(pl.multiple_of(64 * zd, 64), 80)]
        direct.append(send(piece, r3.at[sem], d_s.at[sem], d_r.at[sem], {"dp": yd * 4 + zd * 2 + core}))
    for o in (2, 1, 3):
        columns(o, 1).wait_send()
        columns(o, 2).wait_send()
    wait(back_z)
    back_x = [
        send(
            hold.at[:, lax.rem(x + o, 4)], back.at[pl.ds(x * 4, 4)], bk_s.at[o + 2], bk_r.at[o + 2], x_peer(o)
        )
        for o in (2, 1, 3)
    ]
    back[pl.ds(x * 4, 4)] = hold[:, x]
    pairs_q.append(pair_z(1))

    wait(later)
    sum_o[...] = add(tb[x], ub[0], ub[1], ub[2])
    zs_o[...] = sum_o[pl.ds(pl.multiple_of(64 * (1 - zl), 64), 80), :].astype(BF16)
    pair_o = send(zs_o, zr_o, z_s.at[0], z_r.at[0], zl_peer)

    def four_z(value, hs, hr, width, sem):
        for b in range(4):
            hs[b, 0:72, 0:width] = value[:, width * b : width * b + width].astype(BF16)
        return [
            send(hs.at[lax.rem(zh + o, 4)], hr.at[o - 1], z_s.at[sem + o], z_r.at[sem + o], zh_peer(o))
            for o in (2, 1, 3)
        ]

    window = pl.ds(pl.multiple_of(64 * zl, 64), 80)
    inner = pl.ds(pl.multiple_of(8 * zl, 8), 72)
    pair_o.wait()
    kept_o[...] = sum_o[window, :] + zr_o[...].astype(F32)
    four_o = four_z(kept_o[inner, :], hs_o, hr_o, 72, 0)
    wait(pairs_q)
    for turn in range(2):
        part = lax.rem(turn + x, 3)
        kept_q[part] = sum_q[part, window, :] + zr_q[part].astype(F32)
    wait(direct)
    kept_q[last] = add(s2[y, last, window, :], *(r3[n] for n in range(7)))
    four_q = four_z(jnp.concatenate([kept_q[part, inner, 0:288] for part in range(3)], axis=1), hs_q, hr_q, 216, 6)
    wait(back_x)
    own_d.wait()
    d_x1_ref[...] = (up[...].astype(F32) + back[...].astype(F32)).astype(BF16)
    wait(four_o)
    reso_ref[...] = add(hs_o[zh], hr_o[0], hr_o[1], hr_o[2])
    wait(four_q)
    resq_ref[...] = add(hs_q[zh], hr_q[0], hr_q[1], hr_q[2])


def fused(x, dout, wqkv, wout):
    dma = pltpu.SemaphoreType.DMA

    def buf(*shape, dtype=BF16):
        return pltpu.VMEM(shape, dtype)

    return pl.pallas_call(
        kernel,
        out_shape=[
            jax.ShapeDtypeStruct((16, PX, D), BF16),
            jax.ShapeDtypeStruct((80, 256), F32),
            jax.ShapeDtypeStruct((80, 128), F32),
        ],
        in_specs=[pl.BlockSpec(memory_space=pl.ANY)] * 4,
        out_specs=[pl.BlockSpec(memory_space=pltpu.VMEM)] * 3,
        scratch_shapes=[
            buf(FR, PX, D), buf(D, 3 * D), buf(D, D), buf(16, PX, D),
            buf(TOK, D, dtype=F32), buf(3 * D, TOK, dtype=F32), buf(D, TOK, dtype=F32),
            buf(16, 2, 128, 128, dtype=F32), buf(4, 4, PX, D), buf(4, 4, PX, D), buf(16, PX, D),
            buf(2, HALF, TOK), buf(HALF, 8 * TOK), buf(2, HALF, TOK), buf(HALF, TOK),
            buf(D, TOK), buf(D, TOK), buf(3 * D, TOK), buf(864, 8 * TOK),
            buf(4, 144, D), buf(3, 144, D), buf(4, 144, OW), buf(3, 144, OW),
            buf(144, OW, dtype=F32), buf(80, OW), buf(80, OW), buf(80, OW, dtype=F32),
            buf(4, 80, 128), buf(3, 80, 128),
            buf(4, 3, 144, OW), buf(3, 3, 144, OW), buf(7, 80, OW),
            buf(3, 144, OW, dtype=F32), buf(3, 80, OW), buf(3, 80, OW), buf(3, 80, OW, dtype=F32),
            buf(4, 80, 256), buf(3, 80, 256),
            dma((5,)), dma((16,)), dma((16,)), dma((3,)), dma((3,)), dma((6,)), dma((6,)),
            dma((6,)), dma((6,)), dma((9,)), dma((9,)), dma((10,)), dma((10,)),
            dma((3,)), dma((3,)), dma((6,)), dma((6,)), dma((7,)), dma((7,)), dma((3,)), dma((3,)), dma((10,)), dma((10,)),
        ],
        compiler_params=pltpu.CompilerParams(
            collective_id=1, has_side_effects=True, vmem_limit_bytes=56 * MIB
        ),
    )(x, dout, wqkv, wout)


def finish_kernel(d_x1, resq, reso, out, g_qkv, g_out):
    out[...] = d_x1[...]
    g_qkv[...] = resq[0:72, 0:216] * (1.0 / 256.0)
    g_out[...] = reso[0:72, 0:72] * (1.0 / 256.0)


def finish(d_x1, resq, reso):
    vmem = pl.BlockSpec(memory_space=pltpu.VMEM)
    return pl.pallas_call(
        finish_kernel,
        out_shape=[
            jax.ShapeDtypeStruct((16, PX, D), BF16),
            jax.ShapeDtypeStruct((72, 216), F32),
            jax.ShapeDtypeStruct((72, 72), F32),
        ],
        in_specs=[vmem] * 3,
        out_specs=[vmem] * 3,
    )(d_x1, resq, reso)


def local(x1_pixels, dout_frames, w_qkv, w_out):
    x = x1_pixels.reshape(FR, PX, D)
    dout = dout_frames.reshape(16, PX, D)
    d_x1, g_qkv, g_out = finish(*fused(x, dout, w_qkv, w_out))
    return d_x1.reshape(dout_frames.shape), g_qkv, g_out


def solution(mesh):
    return jax.shard_map(
        local,
        mesh=mesh,
        in_specs=(P("dp", None, "seq", None), P("dp", "seq", None, None), P(), P()),
        out_specs=(P("dp", "seq", None, None), P("dp", "seq"), P("dp", "seq")),
        check_vma=False,
    )
```

```python
import jax
import jax.numpy as jnp
from jax import lax
from jax.experimental import pallas as pl
from jax.experimental.pallas import tpu as pltpu
from jax.sharding import PartitionSpec as P

F32, BF16 = jnp.float32, jnp.bfloat16
EPS = 1e-06
HD = 72
D = 1152
HALF = D // 2
FR = 16
PX = 16
TOK = FR * PX
FACTOR = HD**-0.5
NT = (((1,), (1,)), ((), ()))
TN = (((0,), (0,)), ((), ()))
QW, OW = 896, 384
MIB = 1 << 20


def dot(a, b, dims=None):
    if dims is None:
        return jnp.dot(a, b, preferred_element_type=F32)
    return lax.dot_general(a, b, dims, preferred_element_type=F32)


def to_rows(block):
    return jnp.concatenate([block[:, 8 * p : 8 * p + 8, :].reshape(128, D) for p in range(2)], axis=0)


def from_rows(rows):
    return jnp.concatenate([rows[128 * p : 128 * p + 128].reshape(FR, 8, D) for p in range(2)], axis=1)


def head_scale(v):
    return lax.rsqrt(jnp.sum(v * v, axis=0, keepdims=True) * (1.0 / HD) + EPS)


def forward_head(q, k, v, mask, keep):
    qn, kn, vb = (q * head_scale(q)).astype(BF16), (k * head_scale(k)).astype(BF16), v.astype(BF16)
    out = []
    for p in range(2):
        at = slice(128 * p, 128 * p + 128)
        e = jnp.exp(dot(kn[:, at], qn[:, at], TN) * FACTOR).reshape(FR, 8, 128)
        probs = (e * (mask / jnp.sum(e, axis=0))[None]).reshape(128, 128)
        keep(p, probs)
        out.append(dot(vb[:, at], probs.astype(BF16)))
    return jnp.concatenate(out, axis=1)


def backward_head(q, k, v, ga, probs_of):
    rq, rk = head_scale(q), head_scale(k)
    qn, kn = (q * rq).astype(BF16), (k * rk).astype(BF16)
    vb, gb = v.astype(BF16), ga.astype(BF16)
    out = []
    for p in range(2):
        at = slice(128 * p, 128 * p + 128)
        qh, kh, vh, gh = qn[:, at], kn[:, at], vb[:, at], gb[:, at]
        flat = probs_of(p)
        probs = flat.reshape(FR, 8, 128)
        pb = flat.astype(BF16)
        grad_probs = dot(vh, gh, TN).reshape(FR, 8, 128)
        total = jnp.sum(probs * grad_probs, axis=0)
        gs = (probs * (grad_probs - total[None]) * FACTOR).reshape(128, 128).astype(BF16)
        out.append((dot(kh, gs), dot(qh, gs, NT), dot(gh, pb, NT)))
    gqn, gkn, gv = (jnp.concatenate(pair, axis=1) for pair in zip(*out))
    tq = jnp.sum(gqn * q, axis=0, keepdims=True) * (1.0 / HD)
    tk = jnp.sum(gkn * k, axis=0, keepdims=True) * (1.0 / HD)
    gq = rq * gqn - q * (rq * rq * rq * tq)
    gk = rk * gkn - k * (rk * rk * rk * tk)
    return gq, gk, gv


def add(own, *others):
    value = own.astype(F32)
    for other in others:
        value = value + other.astype(F32)
    return value


def kernel(
    x_hbm, dout_hbm, wqkv_hbm, wout_hbm, d_x1_ref, resq_ref, reso_ref,
    xv, wqkv, wout, up, std, proj, gat, probs, branch, hold, back, nt, nall, at, pa, ut, pu, gp, gall,
    ob, rob, tb, ub, sum_o, zs_o, zr_o, kept_o, hs_o, hr_o,
    s2, r2, r3, sum_q, zs_q, zr_q, kept_q, hs_q, hr_q,
    load, sp_s, sp_r, pair_s, pair_r, bk_s, bk_r, n_s, n_r, gx_s, gx_r, fw_s, fw_r,
    ob_s, ob_r, y_s, y_r, d_s, d_r, x2_s, x2_r, z_s, z_r,
):
    dp, seq = lax.axis_index("dp"), lax.axis_index("seq")
    y, zl, core, x, zh = dp // 4, (dp // 2) % 2, dp % 2, seq // 4, seq % 4

    def seq_peer(o):
        return {"seq": lax.rem(seq + o, 16)}

    def x_peer(o):
        return {"seq": lax.rem(x + o, 4) * 4 + zh}

    def zh_peer(o):
        return {"seq": x * 4 + lax.rem(zh + o, 4)}

    def y_peer(o):
        return {"dp": lax.rem(y + o, 4) * 4 + zl * 2 + core}

    core_peer = {"dp": dp + 1 - 2 * core}
    zl_peer = {"dp": dp + 2 - 4 * zl}

    def send(src, dst, s_sem, r_sem, peer):
        copy = pltpu.make_async_remote_copy(src_ref=src, dst_ref=dst, send_sem=s_sem, recv_sem=r_sem, device_id=peer)
        copy.start()
        return copy

    def wait(copies):
        for copy in copies:
            copy.wait()

    barrier = pltpu.get_barrier_semaphore()
    across = [{"dp": lax.rem(y + o, 4) * 4 + 2 * (1 - zl) + core} for o in range(1, 4)]
    for peer in [seq_peer(o) for o in range(1, 16)] + [y_peer(o) for o in range(1, 4)] + across + [core_peer, zl_peer]:
        pl.semaphore_signal(barrier, inc=1, device_id=peer)
    loads = [
        pltpu.make_async_copy(x_hbm, xv, load.at[0]),
        pltpu.make_async_copy(wqkv_hbm, wqkv, load.at[1]),
        pltpu.make_async_copy(wout_hbm, wout, load.at[2]),
        pltpu.make_async_copy(dout_hbm.at[seq], up.at[seq], load.at[3]),
    ]
    for copy in loads:
        copy.start()
    pl.semaphore_wait(barrier, 23)
    order = (8, 7, 9, 6, 10, 5, 11, 4, 12, 3, 13, 2, 14, 1, 15)
    spread = [
        send(dout_hbm.at[lax.rem(seq + o, 16)], up.at[seq], sp_s.at[o], sp_r.at[o], seq_peer(o)) for o in order
    ]

    loads[0].wait()
    rows = to_rows(xv[...].astype(F32))
    centred = rows - jnp.mean(rows, axis=-1, keepdims=True)
    inverse = lax.rsqrt(jnp.mean(centred * centred, axis=-1, keepdims=True) + EPS)
    standard = centred * inverse
    std[...] = standard
    normed = standard.astype(BF16)
    standard_t = standard.T
    for c in range(2):
        nt[c] = jnp.concatenate(
            [standard_t[HD * (2 * b + c) : HD * (2 * b + c + 1)] for b in range(8)], axis=0
        ).astype(BF16)
    pair_n = send(nt.at[1 - core], nall.at[:, TOK : 2 * TOK], pair_s.at[0], pair_r.at[0], core_peer)
    nall[:, 0:TOK] = nt[core]
    right, left = x_peer(1), x_peer(3)
    pair_n.wait()
    own_rows, pair_rows = nall.at[:, 0:TOK], nall.at[:, TOK : 2 * TOK]
    rows_first = [
        send(own_rows, nall.at[:, 2 * TOK : 3 * TOK], n_s.at[0], n_r.at[0], right),
        send(pair_rows, nall.at[:, 7 * TOK : 8 * TOK], n_s.at[1], n_r.at[1], left),
    ]
    loads[1].wait()
    for t in range(3):
        proj[D * t : D * t + D, :] = dot(normed, wqkv[:, D * t : D * t + D]).T

    mask = (
        lax.broadcasted_iota(jnp.int32, (8, 128), 0) == lax.broadcasted_iota(jnp.int32, (8, 128), 1) % 8
    ).astype(F32)

    def forward_group(i, carry):
        base = pl.multiple_of(i * 288, 288)
        blocks = [proj[pl.ds(pl.multiple_of(D * t + base, 288), 288), :] for t in range(3)]
        heads = []
        for h in range(4):

            def keep(p, value, h=h):
                probs[i * 4 + h, p] = value

            heads.append(forward_head(*(b[HD * h : HD * h + HD] for b in blocks), mask, keep))
        half = pl.multiple_of(i * 144, 144)
        for c in range(2):
            at[c, pl.ds(half, 144), :] = jnp.concatenate([heads[c], heads[c + 2]], axis=0).astype(BF16)
        return carry

    lax.fori_loop(0, 4, forward_group, 0)
    pair_a = send(at.at[1 - core], pa, pair_s.at[1], pair_r.at[1], core_peer)

    wait(rows_first)
    rows_on = [
        send(nall.at[:, 2 * TOK : 3 * TOK], nall.at[:, 4 * TOK : 5 * TOK], n_s.at[2], n_r.at[2], right),
        send(nall.at[:, 7 * TOK : 8 * TOK], nall.at[:, 5 * TOK : 6 * TOK], n_s.at[3], n_r.at[3], left),
        send(pair_rows, nall.at[:, 3 * TOK : 4 * TOK], n_s.at[4], n_r.at[4], right),
        send(own_rows, nall.at[:, 6 * TOK : 7 * TOK], n_s.at[5], n_r.at[5], left),
    ]
    hs_o[...] = jnp.zeros_like(hs_o)
    hs_q[...] = jnp.zeros_like(hs_q)

    loads[2].wait()
    loads[3].wait()
    wait(spread)
    up_t = to_rows(up[...].astype(F32)).T.astype(BF16)
    ut[...] = up_t
    pair_u = send(ut, pu, pair_s.at[2], pair_r.at[2], core_peer)
    gat[...] = dot(wout[...], up_t)
    wait([pair_a, pair_u])

    own_a = at[core]
    for n in range(3):
        cols = slice(OW * n, OW * n + OW)
        val = (dot(own_a, ut[cols, :], NT) + dot(pa[...], pu[cols, :], NT)).astype(BF16)
        for r in range(4):
            ob[r, :, cols] = val[144 * r : 144 * r + 144]
    out_y = [
        send(ob.at[lax.rem(y + o, 4)], rob.at[o - 1], ob_s.at[o - 1], ob_r.at[o - 1], y_peer(o)) for o in (2, 1, 3)
    ]


    def columns(o, turn):
        xd = lax.rem(x + o, 4)
        part = lax.rem(turn + xd, 3)
        return pltpu.make_async_remote_copy(
            src_ref=gp.at[pl.ds(pl.multiple_of((3 * xd + part) * 288, 32), 288)],
            dst_ref=gall.at[pl.ds(pl.multiple_of(part * 288, 32), 288), 2 * o * TOK : (2 * o + 1) * TOK],
            send_sem=gx_s.at[3 * (o - 1) + turn],
            recv_sem=gx_r.at[3 * (o - 1) + turn],
            device_id=x_peer(o),
        )

    def issue(turn):
        for o in (2, 1, 3):
            columns(o, turn).start()

    def backward_group(i, carry):
        base = pl.multiple_of(i * 288, 288)
        blocks = [proj[pl.ds(pl.multiple_of(D * t + base, 288), 288), :] for t in range(3)]
        blocks.append(gat[pl.ds(base, 288), :])
        heads = [
            backward_head(*(b[HD * h : HD * h + HD] for b in blocks), lambda p, h=h: probs[i * 4 + h, p])
            for h in range(4)
        ]
        for t in range(3):
            gp[pl.ds(pl.multiple_of(D * t + base, 288), 288), :] = jnp.concatenate(
                [h[t] for h in heads], axis=0
            ).astype(BF16)
        return carry

    lax.fori_loop(0, 2, backward_group, 0)
    issue(0)
    lax.fori_loop(2, 4, backward_group, 0)
    issue(1)
    mine = gp.at[pl.ds(pl.multiple_of(x * 864, 32), 864)]
    own_g = pltpu.make_async_copy(mine, gall.at[0:864, 0:TOK], load.at[4])
    own_g.start()
    pair_g = send(mine, gall.at[0:864, TOK : 2 * TOK], fw_s.at[9], fw_r.at[9], core_peer)

    gn = dot(wqkv[...], gp[...]).T
    standard = std[...]
    value = inverse * (
        gn
        - jnp.mean(gn, axis=-1, keepdims=True)
        - standard * jnp.mean(gn * standard, axis=-1, keepdims=True)
    )
    branch[...] = from_rows(value).astype(BF16).reshape(4, 4, PX, D)
    back_z = [
        send(branch.at[:, lax.rem(zh + o, 4)], hold.at[zh], bk_s.at[o - 1], bk_r.at[o - 1], zh_peer(o))
        for o in (2, 1, 3)
    ]
    hold[zh] = branch[:, zh]

    for o in (2, 1, 3):
        columns(o, 0).wait_send()
    issue(2)

    wait(out_y)
    val = add(ob[y], rob[0], rob[1], rob[2]).astype(BF16)
    for b in range(4):
        tb[b, :, 0:288] = val[:, 288 * b : 288 * b + 288]
        tb[b, :, 288:OW] = jnp.zeros((144, OW - 288), BF16)

    own_d = pltpu.make_async_copy(dout_hbm, up, load.at[3])
    own_d.start()

    wait(rows_on + [pair_g])
    own_g.wait()
    sums_y = []

    def pair_z(turn):
        wait(sums_y[turn])
        part = lax.rem(turn + x, 3)
        sum_q[part] = add(s2[y, part], r2[0, part], r2[1, part], r2[2, part])
        zs_q[part] = sum_q[part, pl.ds(pl.multiple_of(64 * (1 - zl), 64), 80), :].astype(BF16)
        return send(zs_q.at[part], zr_q.at[part], z_s.at[turn + 4], z_r.at[turn + 4], zl_peer)

    pairs_q = []
    for turn in range(3):
        part = lax.rem(turn + x, 3)
        rows = pl.ds(pl.multiple_of(part * 288, 32), 288)
        forwards = []
        for o in (1, 3, 2):
            columns(o, turn).wait_recv()
            sem = (o - 1) * 3 + turn
            forwards.append(
                send(
                    gall.at[rows, 2 * o * TOK : (2 * o + 1) * TOK],
                    gall.at[rows, (2 * o + 1) * TOK : (2 * o + 2) * TOK],
                    fw_s.at[sem], fw_r.at[sem], core_peer,
                )
            )
        wait(forwards)
        val = dot(nall[...], gall[rows, :], NT)
        val = jnp.concatenate([val, jnp.zeros((HALF, OW - 288), F32)], axis=1).astype(BF16)
        for b in range(4):
            s2[b, part] = val[144 * b : 144 * b + 144]
        if turn < 2:
            sums_y.append(
                [
                    send(
                        s2.at[lax.rem(y + o, 4), part], r2.at[o - 1, part],
                        y_s.at[3 * turn + o - 1], y_r.at[3 * turn + o - 1], y_peer(o),
                    )
                    for o in (2, 1, 3)
                ]
            )
        if turn == 1:
            pairs_q.append(pair_z(0))
            later = [
                send(tb.at[lax.rem(x + o, 4)], ub.at[o - 1], x2_s.at[o - 1], x2_r.at[o - 1], x_peer(o)) for o in (2, 1, 3)
            ]
    last = lax.rem(2 + x, 3)
    direct = []
    for o, oz in ((2, 1), (2, 0), (1, 1), (1, 0), (3, 1), (3, 0), (0, 1)):
        yd, zd, sem = lax.rem(y + o, 4), (zl if oz == 0 else 1 - zl), 2 * o + oz - 1
        piece = s2.at[yd, last, pl.ds(pl.multiple_of(64 * zd, 64), 80)]
        direct.append(send(piece, r3.at[sem], d_s.at[sem], d_r.at[sem], {"dp": yd * 4 + zd * 2 + core}))
    for o in (2, 1, 3):
        columns(o, 1).wait_send()
        columns(o, 2).wait_send()
    wait(back_z)
    back_x = [
        send(
            hold.at[:, lax.rem(x + o, 4)], back.at[pl.ds(x * 4, 4)], bk_s.at[o + 2], bk_r.at[o + 2], x_peer(o)
        )
        for o in (2, 1, 3)
    ]
    back[pl.ds(x * 4, 4)] = hold[:, x]
    pairs_q.append(pair_z(1))

    wait(later)
    sum_o[...] = add(tb[x], ub[0], ub[1], ub[2])
    zs_o[...] = sum_o[pl.ds(pl.multiple_of(64 * (1 - zl), 64), 80), :].astype(BF16)
    pair_o = send(zs_o, zr_o, z_s.at[0], z_r.at[0], zl_peer)

    def four_z(value, hs, hr, width, sem):
        for b in range(4):
            hs[b, 0:72, 0:width] = value[:, width * b : width * b + width].astype(BF16)
        return [
            send(hs.at[lax.rem(zh + o, 4)], hr.at[o - 1], z_s.at[sem + o], z_r.at[sem + o], zh_peer(o))
            for o in (2, 1, 3)
        ]

    window = pl.ds(pl.multiple_of(64 * zl, 64), 80)
    inner = pl.ds(pl.multiple_of(8 * zl, 8), 72)
    pair_o.wait()
    kept_o[...] = sum_o[window, :] + zr_o[...].astype(F32)
    four_o = four_z(kept_o[inner, :], hs_o, hr_o, 72, 0)
    wait(pairs_q)
    for turn in range(2):
        part = lax.rem(turn + x, 3)
        kept_q[part] = sum_q[part, window, :] + zr_q[part].astype(F32)
    wait(direct)
    kept_q[last] = add(s2[y, last, window, :], *(r3[n] for n in range(7)))
    four_q = four_z(jnp.concatenate([kept_q[part, inner, 0:288] for part in range(3)], axis=1), hs_q, hr_q, 216, 6)
    wait(back_x)
    own_d.wait()
    d_x1_ref[...] = (up[...].astype(F32) + back[...].astype(F32)).astype(BF16)
    wait(four_o)
    reso_ref[...] = add(hs_o[zh], hr_o[0], hr_o[1], hr_o[2])
    wait(four_q)
    resq_ref[...] = add(hs_q[zh], hr_q[0], hr_q[1], hr_q[2])


def fused(x, dout, wqkv, wout):
    dma = pltpu.SemaphoreType.DMA

    def buf(*shape, dtype=BF16):
        return pltpu.VMEM(shape, dtype)

    return pl.pallas_call(
        kernel,
        out_shape=[
            jax.ShapeDtypeStruct((16, PX, D), BF16),
            jax.ShapeDtypeStruct((80, 256), F32),
            jax.ShapeDtypeStruct((80, 128), F32),
        ],
        in_specs=[pl.BlockSpec(memory_space=pl.ANY)] * 4,
        out_specs=[pl.BlockSpec(memory_space=pltpu.VMEM)] * 3,
        scratch_shapes=[
            buf(FR, PX, D), buf(D, 3 * D), buf(D, D), buf(16, PX, D),
            buf(TOK, D, dtype=F32), buf(3 * D, TOK, dtype=F32), buf(D, TOK, dtype=F32),
            buf(16, 2, 128, 128, dtype=F32), buf(4, 4, PX, D), buf(4, 4, PX, D), buf(16, PX, D),
            buf(2, HALF, TOK), buf(HALF, 8 * TOK), buf(2, HALF, TOK), buf(HALF, TOK),
            buf(D, TOK), buf(D, TOK), buf(3 * D, TOK), buf(864, 8 * TOK),
            buf(4, 144, D), buf(3, 144, D), buf(4, 144, OW), buf(3, 144, OW),
            buf(144, OW, dtype=F32), buf(80, OW), buf(80, OW), buf(80, OW, dtype=F32),
            buf(4, 80, 128), buf(3, 80, 128),
            buf(4, 3, 144, OW), buf(3, 3, 144, OW), buf(7, 80, OW),
            buf(3, 144, OW, dtype=F32), buf(3, 80, OW), buf(3, 80, OW), buf(3, 80, OW, dtype=F32),
            buf(4, 80, 256), buf(3, 80, 256),
            dma((5,)), dma((16,)), dma((16,)), dma((3,)), dma((3,)), dma((6,)), dma((6,)),
            dma((6,)), dma((6,)), dma((9,)), dma((9,)), dma((10,)), dma((10,)),
            dma((3,)), dma((3,)), dma((6,)), dma((6,)), dma((7,)), dma((7,)), dma((3,)), dma((3,)), dma((10,)), dma((10,)),
        ],
        compiler_params=pltpu.CompilerParams(
            collective_id=1, has_side_effects=True, vmem_limit_bytes=56 * MIB
        ),
    )(x, dout, wqkv, wout)


def finish_kernel(resq, reso, g_qkv, g_out):
    g_qkv[...] = resq[0:72, 0:216] * (1.0 / 256.0)
    g_out[...] = reso[0:72, 0:72] * (1.0 / 256.0)


def finish(resq, reso):
    vmem = pl.BlockSpec(memory_space=pltpu.VMEM)
    return pl.pallas_call(
        finish_kernel,
        out_shape=[
            jax.ShapeDtypeStruct((72, 216), F32),
            jax.ShapeDtypeStruct((72, 72), F32),
        ],
        in_specs=[vmem] * 2,
        out_specs=[vmem] * 2,
    )(resq, reso)


def local(x1_pixels, dout_frames, w_qkv, w_out):
    x = x1_pixels.reshape(FR, PX, D)
    dout = dout_frames.reshape(16, PX, D)
    d_x1, resq, reso = fused(x, dout, w_qkv, w_out)
    g_qkv, g_out = finish(resq, reso)
    return d_x1.reshape(dout_frames.shape), g_qkv, g_out


def solution(mesh):
    return jax.shard_map(
        local,
        mesh=mesh,
        in_specs=(P("dp", None, "seq", None), P("dp", "seq", None, None), P(), P()),
        out_specs=(P("dp", "seq", None, None), P("dp", "seq"), P("dp", "seq")),
        check_vma=False,
    )
```
